32 devices in a mesh: kp: 8 (over y, x, core), ka: 4 (over z).
Axes of the slice: x: 2, y: 2, z: 4, core: 2. Of those that a mesh axis runs over, the one named last changes fastest.
Arguments:
- band_form: bfloat16 [16, 24, 2048], P('ka'), may hold values from -0.71875 to 0.71875
- interp_coef: bfloat16 [16, 128, 128], P('ka'), may hold values from -0.5 to 0.5
- screen: bfloat16 [16, 2048, 32], P('ka', 'kp'), may hold values from -0.3984375 to 0.3984375
- coulomb: float32 [2048], replicated, may hold values from 0.3 to 3
- shift_map: int32 [16, 2048], replicated, may hold values from 0 to 2047, each once within a row
- grid_order: int32 [16], replicated, may hold values from 0 to 15, each once
- energies: float32 [2048], P('ka'), may hold values from 0.09050967 to 0.271529
- initial: float32 [2048, 64], P('ka'), may hold values from -6 to 6
Outputs:
- kernel: bfloat16 [2048, 2048], P('ka', 'kp')
- subspace: float32 [2048, 64], P('ka')
The draws below stay inside these ranges and needn't reach their ends.
All inputs are finite; a program needn't handle non-finite values.
Results may differ from the reference program's by a relative error of at most 0.02.
Values may be sent and summed in bfloat16 or wider, within the bound.
A program may use at most 64 MiB of HBM per device.

```python
import math
import jax
import jax.numpy as jnp
from jax import lax

NV = 8
NC = 16
NG = 2048
NE = 32
NVEC = 64
STEPS = 2
GRID_Y = 8
NB = 24
NVC = 128
NK = 16
NQ = 16
N = 2048


def shard_levels(stream_key, extent, split, low, largest):
    loudness = 1.0
    for axis_at, parts in split:
        draws = jax.random.uniform(jax.random.fold_in(jax.random.fold_in(stream_key, 6), axis_at), (parts,), jnp.float32, low / len(split), largest / len(split))
        loudness = loudness * jnp.repeat(jnp.exp(draws), extent[axis_at] // parts).reshape((-1,) + (1,) * (len(extent) - 1 - axis_at))
    return loudness


def centred(rng, dims, scale, bound, split=(), held_as=jnp.bfloat16):
    level = shard_levels(rng, dims, split, -0.22, 0.18) if split else 1.0
    entries = jax.random.normal(rng, dims, jnp.float32) * scale * level
    return jnp.minimum(jnp.maximum(entries, -bound), bound).astype(held_as)


def setup_inputs(seed: int = 0) -> dict:
    arg_keys = jax.random.split(jax.random.key(seed), 9)
    return {
        "band_form": centred(arg_keys[0], (NK, NB, NG), (0.12 * (2048 // NG) ** 0.125), 0.71875, ((0, 4),)),
        "interp_coef": centred(arg_keys[1], (NK, NVC, NVC), NVC ** -0.5, 0.5, ((0, 4),)),
        "screen": centred(arg_keys[2], (NQ, NG, NE), 0.0625, 0.3984375, ((0, 4), (1, 8))),
        "coulomb": jnp.clip(jnp.exp(jax.random.uniform(arg_keys[3], (NG,), jnp.float32, math.log(0.3), math.log(3.0))), 0.3, 3.0),
        "shift_map": jax.vmap(lambda own: jax.random.permutation(own, NG))(jax.random.split(arg_keys[4], NQ)).reshape((NQ, NG)).astype(jnp.int32),
        "grid_order": jax.random.permutation(arg_keys[5], NK).astype(jnp.int32),
        "energies": jnp.clip(0.09050967 + 0.18101932 * jax.random.uniform(arg_keys[6], (N,), jnp.float32) ** shard_levels(arg_keys[6], (N,), ((0, 4),), -0.2, 0.2), 0.09050967, 0.271529),
        "initial": centred(arg_keys[7], (N, NVEC), 1.0, 6.0, ((0, 4),), jnp.float32),
    }


def pair_block(near_form, mapped, near_coef, far_coef, screen_cols, coulomb):
    valence = (near_form[:NV, None, :].astype(jnp.float32) * mapped[None, :NV, :].astype(jnp.float32)).reshape(NV * NV, -1).astype(jnp.bfloat16)
    conduction = (near_form[NV:, None, :].astype(jnp.float32) * mapped[None, NV:, :].astype(jnp.float32)).reshape(NC * NC, -1).astype(jnp.bfloat16)
    scaled = (coulomb[None, :] * valence.astype(jnp.float32)).astype(jnp.bfloat16)
    direct = jnp.dot(conduction.astype(jnp.float32), scaled.T.astype(jnp.float32), preferred_element_type=jnp.float32)
    left = jnp.dot(conduction.astype(jnp.float32), screen_cols.astype(jnp.float32), preferred_element_type=jnp.float32)
    right = jnp.dot(valence.astype(jnp.float32), screen_cols.astype(jnp.float32), preferred_element_type=jnp.float32)
    direct = direct + jnp.dot(left.astype(jnp.float32), right.T.astype(jnp.float32), precision=lax.Precision.HIGHEST, preferred_element_type=jnp.float32)
    block = direct.reshape(NC, NC, NV, NV).transpose(2, 0, 3, 1).reshape(NV * NC, NV * NC).astype(jnp.bfloat16)
    half = jnp.dot(block.astype(jnp.float32), far_coef.astype(jnp.float32), preferred_element_type=jnp.float32).astype(jnp.bfloat16)
    return jnp.dot(near_coef.T.astype(jnp.float32), half.astype(jnp.float32), preferred_element_type=jnp.float32).astype(jnp.bfloat16)

def reference(band_form, interp_coef, screen, coulomb, shift_map, grid_order, energies, initial):
    grid_x = NK // GRID_Y
    cell_x = grid_order // GRID_Y
    cell_y = grid_order % GRID_Y
    pairs = NV * NC

    def kernel_row(point):
        transfers = ((cell_x[point] - cell_x) % grid_x * GRID_Y + (cell_y[point] - cell_y) % GRID_Y).astype(jnp.int32)
        maps = jnp.take(shift_map, transfers, axis=0)
        mapped = jnp.take_along_axis(band_form, maps[:, None, :], axis=2)
        columns = jnp.take(screen, transfers, axis=0)
        blocks = jax.vmap(pair_block, in_axes=(None, 0, None, 0, 0, None))(band_form[point], mapped, interp_coef[point], interp_coef, columns, coulomb)
        return blocks.transpose(1, 0, 2).reshape(pairs, NK * pairs)
    kernel = lax.map(kernel_row, jnp.arange(NK, dtype=jnp.int32)).reshape(NK * pairs, NK * pairs)
    vectors = initial
    for repeat in range(STEPS):
        images = energies[:, None] * vectors + jnp.dot(kernel.astype(jnp.float32), vectors.astype(jnp.bfloat16).astype(jnp.float32), preferred_element_type=jnp.float32)
        correlation = jnp.dot(images.T.astype(jnp.float32), images.astype(jnp.float32), precision=lax.Precision.HIGHEST, preferred_element_type=jnp.float32) / (NK * pairs)
        factor = jnp.linalg.cholesky(correlation)
        vectors = jax.scipy.linalg.solve_triangular(factor, images.T, lower=True).T
    return (kernel, vectors)
```

```python
import functools

import jax
import jax.numpy as jnp
from jax import lax
from jax.experimental import pallas as pl
from jax.experimental.pallas import tpu as pltpu
from jax.sharding import PartitionSpec as P

NV = 8
NC = 16
STEPS = 2
GRID_Y = 8
LANES = 128
CHUNK = 512
MESH = pl.DeviceIdType.MESH
VMEM = pl.BlockSpec(memory_space=pltpu.VMEM)
SMEM = pl.BlockSpec(memory_space=pltpu.SMEM)
NT = (((1,), (1,)), ((), ()))
F32 = jnp.float32
BF16 = jnp.bfloat16


def exchange_kernel(
    size_ka, size_kp, form, coef, start, cols,
    far_form, far_coef, far_start, all_cols,
    up_sem, down_sem, far_sem,
    z_send, z_recv, plane_send, plane_recv, core_send, core_recv,
):
    ka, kp = lax.axis_index("ka"), lax.axis_index("kp")
    chips = size_kp // 2
    chip, core = kp // 2, kp % 2
    near, far = form.shape[0], far_form.shape[0]
    rows = cols.shape[0]
    owner = kp * far // near
    offset = kp * far % near

    barrier = pltpu.get_barrier_semaphore()

    def greet_z(d, carry):
        pl.semaphore_signal(barrier, inc=1, device_id={"ka": (ka + d) % size_ka}, device_id_type=MESH)
        return carry

    def greet_plane(d, carry):
        other = (chip + d) % chips * 2 + core
        pl.semaphore_signal(barrier, inc=1, device_id={"kp": other}, device_id_type=MESH)
        return carry

    lax.fori_loop(1, size_ka, greet_z, 0)
    lax.fori_loop(1, chips, greet_plane, 0)
    pl.semaphore_signal(barrier, inc=1, device_id={"kp": chip * 2 + 1 - core}, device_id_type=MESH)
    pl.semaphore_wait(barrier, size_ka - 1 + chips - 1 + 1)

    pieces = [far_form.at[i] for i in range(far)] + [far_coef, far_start]

    def far_copy(i, sem, target):
        return pltpu.make_async_remote_copy(
            src_ref=pieces[i], dst_ref=pieces[i], send_sem=sem.at[i], recv_sem=far_sem.at[i],
            device_id={"ka": target}, device_id_type=MESH,
        )

    goes_up = (ka >= owner) & (ka < size_ka - 1)
    goes_down = (ka <= owner) & (ka > 0)
    above, below = lax.rem(ka + 1, size_ka), lax.rem(ka + size_ka - 1, size_ka)

    def part(z, p):
        return all_cols.at[z, pl.ds(pl.multiple_of(p * rows, rows), rows), :]

    def z_copy(z, target):
        return pltpu.make_async_remote_copy(
            src_ref=part(z, kp), dst_ref=part(z, kp), send_sem=z_send.at[target],
            recv_sem=z_recv.at[z], device_id={"ka": target}, device_id_type=MESH,
        )

    def plane_copy(z, source, target):
        ref = part(z, source * 2 + core)
        return pltpu.make_async_remote_copy(
            src_ref=ref, dst_ref=ref, send_sem=plane_send.at[z, target],
            recv_sem=plane_recv.at[z, source],
            device_id={"kp": target * 2 + core}, device_id_type=MESH,
        )

    def core_copy(z, c, from_core):
        ref = part(z, c * 2 + from_core)
        return pltpu.make_async_remote_copy(
            src_ref=ref, dst_ref=ref, send_sem=core_send.at[z, c], recv_sem=core_recv.at[z, c],
            device_id={"kp": chip * 2 + 1 - core}, device_id_type=MESH,
        )

    @pl.when(ka == owner)
    def _():
        far_form[...] = form[pl.ds(offset, far)]
        far_coef[...] = coef[pl.ds(offset, far)]
        far_start[...] = start[pl.ds(offset, far)]

    all_cols[ka, pl.ds(pl.multiple_of(kp * rows, rows), rows), :] = cols[...]

    def spread(z):
        def to_plane(d, carry):
            plane_copy(z, chip, (chip + d) % chips).start()
            return carry

        lax.fori_loop(1, chips, to_plane, 0)
        core_copy(z, chip, core).start()

    def forward(i):
        @pl.when(goes_up)
        def _():
            far_copy(i, up_sem, above).start()

        @pl.when(goes_down)
        def _():
            far_copy(i, down_sem, below).start()

    @pl.when(ka == owner)
    def _():
        for i in range(len(pieces)):
            forward(i)

    def to_z(d, carry):
        z_copy(ka, (ka + d) % size_ka).start()
        return carry

    lax.fori_loop(1, size_ka, to_z, 0)
    spread(ka)

    @pl.when(ka != owner)
    def _():
        for i in range(len(pieces)):
            far_copy(i, up_sem, above).wait_recv()
            forward(i)

    def from_z(d, carry):
        z = (ka + size_ka - d) % size_ka
        z_copy(z, above).wait_recv()
        spread(z)
        return carry

    lax.fori_loop(1, size_ka, from_z, 0)

    def from_plane(d, carry):
        z = (ka + size_ka - d) % size_ka

        def one(e, inner):
            c = (chip + chips - e) % chips
            plane_copy(z, c, (chip + e) % chips).wait_recv()
            core_copy(z, c, core).start()
            return inner

        return lax.fori_loop(1, chips, one, carry)

    lax.fori_loop(0, size_ka, from_plane, 0)

    def finish(n, carry):
        z, c = n // chips, n % chips
        core_copy(z, c, 1 - core).wait_recv()
        core_copy(z, c, core).wait_send()
        return carry

    lax.fori_loop(0, size_ka * chips, finish, 0)

    def finish_plane(n, carry):
        z, e = n // (chips - 1), n % (chips - 1) + 1
        plane_copy(z, chip, (chip + e) % chips).wait_send()
        return carry

    lax.fori_loop(0, size_ka * (chips - 1), finish_plane, 0)

    def finish_z(d, carry):
        z_copy(ka, (ka + d) % size_ka).wait_send()
        return carry

    lax.fori_loop(1, size_ka, finish_z, 0)
    for i in range(len(pieces)):
        @pl.when(goes_up)
        def _():
            far_copy(i, up_sem, above).wait_send()

        @pl.when(goes_down)
        def _():
            far_copy(i, down_sem, below).wait_send()


def exchange(size_ka, size_kp, far, form, coef, start, cols):
    chips = size_kp // 2
    pieces = far + 2
    dma = pltpu.SemaphoreType.DMA
    return pl.pallas_call(
        functools.partial(exchange_kernel, size_ka, size_kp),
        out_shape=(
            jax.ShapeDtypeStruct((far,) + form.shape[1:], BF16),
            jax.ShapeDtypeStruct((far,) + coef.shape[1:], BF16),
            jax.ShapeDtypeStruct((far,) + start.shape[1:], BF16),
            jax.ShapeDtypeStruct((size_ka, cols.shape[0] * size_kp, cols.shape[1]), BF16),
        ),
        in_specs=[VMEM] * 4,
        out_specs=(VMEM,) * 4,
        scratch_shapes=[
            dma((pieces,)), dma((pieces,)), dma((pieces,)),
            dma((size_ka,)), dma((size_ka,)),
            dma((size_ka, chips)), dma((size_ka, chips)),
            dma((size_ka, chips)), dma((size_ka, chips)),
        ],
        compiler_params=pltpu.CompilerParams(
            collective_id=0, has_side_effects=True, vmem_limit_bytes=48 * 2**20
        ),
    )(form, coef, start, cols)


def blocks_kernel(
    near, far, group, transfers, form, far_form, coef_t, far_coef, all_cols, coulomb, shift_map,
    out, flat, direct, packed,
):
    waves = form.shape[2]
    pieces = waves // LANES
    bands = NV + NC
    per_owner = all_cols.shape[2] // group
    flat[...] = jnp.zeros_like(flat)
    for f in range(far):
        for h in range(pieces):
            flat[f, h, 0:bands, :] = far_form[f, :, h * LANES : (h + 1) * LANES]

    def one_pair(n, carry):
        k, f = n // far, n % far
        q = transfers[n]
        source = flat[f].reshape(pieces * flat.shape[2], LANES)
        height = flat.shape[2]
        owner = q // per_owner
        total = jnp.zeros((NV * NV, NC * NC), F32)
        left = jnp.zeros((NC * NC, all_cols.shape[2]), F32)
        right = jnp.zeros((NV * NV, all_cols.shape[2]), F32)
        for s in range(0, waves, CHUNK):
            index = shift_map[q, :, s : s + CHUNK]
            low = index & (LANES - 1)
            high = index >> 7
            one_hot = jnp.where(
                lax.broadcasted_iota(jnp.int32, (LANES, CHUNK), 0) == low, 1.0, 0.0
            ).astype(BF16)
            spread = jnp.dot(source, one_hot, preferred_element_type=F32)
            mapped = spread[0:bands]
            for h in range(1, pieces):
                mapped = jnp.where(high == h, spread[h * height : h * height + bands], mapped)
            near_form = form[k, :, s : s + CHUNK].astype(F32)
            valence = jnp.concatenate(
                [near_form[v : v + 1] * mapped[0:NV] for v in range(NV)], axis=0
            ).astype(BF16)
            conduction = jnp.concatenate(
                [near_form[NV + c : NV + c + 1] * mapped[NV:] for c in range(NC)], axis=0
            ).astype(BF16)
            scaled = (coulomb[:, s : s + CHUNK] * valence.astype(F32)).astype(BF16)
            columns = all_cols[owner, s : s + CHUNK, :]
            total += lax.dot_general(scaled, conduction, NT, preferred_element_type=F32)
            left += jnp.dot(conduction, columns, preferred_element_type=F32)
            right += jnp.dot(valence, columns, preferred_element_type=F32)
        lane = lax.broadcasted_iota(jnp.int32, right.shape, 1)
        right = jnp.where(lane // group == q % per_owner, right, 0.0)
        total += lax.dot_general(
            right, left, NT, precision=lax.Precision.HIGHEST, preferred_element_type=F32
        )
        rows = NV * NV
        direct[pl.ds(pl.multiple_of(n * rows, rows), rows), :] = total.astype(BF16)
        return carry

    pairs = near * far
    lax.fori_loop(0, pairs, one_pair, 0)

    all_rows = pairs * NV * NV
    row = lax.broadcasted_iota(jnp.int32, (all_rows, LANES), 0)
    lane = lax.broadcasted_iota(jnp.int32, (all_rows, LANES), 1)
    keep = row % NV == lane // NC
    sum_row = lax.broadcasted_iota(jnp.int32, (pairs * NV, all_rows), 0)
    sum_col = lax.broadcasted_iota(jnp.int32, (pairs * NV, all_rows), 1)
    sums = jnp.where(sum_col // NV == sum_row, 1.0, 0.0).astype(BF16)
    pick_row = lax.broadcasted_iota(jnp.int32, (LANES, LANES), 0)
    pick_lane = lax.broadcasted_iota(jnp.int32, (LANES, LANES), 1)
    per_half = LANES // NC
    for c in range(NC):
        pick = jnp.where(
            (pick_row // NC == c % per_half) & (pick_row % NC == pick_lane % NC), 1.0, 0.0
        ).astype(BF16)
        half_at = c // per_half * LANES
        wide = jnp.dot(direct[:, half_at : half_at + LANES], pick, preferred_element_type=F32)
        wide = jnp.where(keep, wide, 0.0).astype(BF16)
        rows = jnp.dot(sums, wide, preferred_element_type=F32)
        packed[:, c * NV : (c + 1) * NV, :] = rows.reshape(pairs, NV, LANES)
    side = NV * NC
    for k in range(near):
        for f in range(far):
            block = packed[k * far + f].astype(BF16)
            half = jnp.dot(block, far_coef[f], preferred_element_type=F32).astype(BF16)
            out[k * side : (k + 1) * side, f * side : (f + 1) * side] = jnp.dot(
                coef_t[k], half, preferred_element_type=F32
            ).astype(BF16)


def blocks(near, far, group, transfers, form, far_form, coef_t, far_coef, all_cols, coulomb, shift_map):
    waves = form.shape[2]
    side = NV * NC
    pairs = near * far
    return pl.pallas_call(
        functools.partial(blocks_kernel, near, far, group),
        out_shape=jax.ShapeDtypeStruct((near * side, far * side), BF16),
        in_specs=[SMEM] + [VMEM] * 7,
        out_specs=VMEM,
        scratch_shapes=[
            pltpu.VMEM((far, waves // LANES, 32, LANES), BF16),
            pltpu.VMEM((pairs * NV * NV, NC * NC), BF16),
            pltpu.VMEM((pairs, side, LANES), F32),
        ],
        compiler_params=pltpu.CompilerParams(vmem_limit_bytes=48 * 2**20),
    )(transfers, form, far_form, coef_t, far_coef, all_cols, coulomb, shift_map)


def inverse_factor(matrix):
    size = matrix.shape[0]
    row = lax.broadcasted_iota(jnp.int32, matrix.shape, 0)
    lane = lax.broadcasted_iota(jnp.int32, matrix.shape, 1)
    work = jnp.where(lane == row + size, 1.0, matrix)
    for j in range(size - 1):
        pivot_row = work[j : j + 1, :]
        scaled_row = pivot_row / pivot_row[:, j : j + 1]
        work = work - jnp.where(row > j, work[:, j : j + 1], 0.0) * scaled_row
    diagonal = jnp.sum(jnp.where(lane == row, work, 0.0), axis=1, keepdims=True)
    return jnp.where(lane >= size, work * lax.rsqrt(diagonal), 0.0)


def subspace_kernel(
    size_ka, size_kp, kernel, far_start, energies, start, out,
    product, image, far_image, far_bf16, received, correlations,
    rs_send, rs_recv, ag_send, ag_recv, z_send, z_recv, far_send, far_recv,
):
    ka, kp = lax.axis_index("ka"), lax.axis_index("kp")
    vectors, rows = start.shape
    far, _, side = far_start.shape
    near = rows // side
    owner = kp * far // near
    offset = kp * far % near
    row_groups = vectors // 8
    lane_groups = size_kp // row_groups
    width = rows // lane_groups
    total_rows = rows * size_ka

    barrier = pltpu.get_barrier_semaphore()

    def greet_z(d, carry):
        pl.semaphore_signal(barrier, inc=1, device_id={"ka": (ka + d) % size_ka}, device_id_type=MESH)
        return carry

    def greet_plane(d, carry):
        pl.semaphore_signal(barrier, inc=1, device_id={"kp": (kp + d) % size_kp}, device_id_type=MESH)
        return carry

    lax.fori_loop(1, size_ka, greet_z, 0)
    lax.fori_loop(1, size_kp, greet_plane, 0)

    def chunk(p):
        return (
            pl.ds(pl.multiple_of(p // lane_groups * 8, 8), 8),
            pl.ds(pl.multiple_of(p % lane_groups * width, width), width),
        )

    own_rows, own_lanes = chunk(kp)
    padding = jnp.zeros((vectors, rows), F32)

    for step in range(STEPS):
        def rs_copy(source, target):
            return pltpu.make_async_remote_copy(
                src_ref=product.at[step].at[chunk(target)],
                dst_ref=received.at[step, source],
                send_sem=rs_send.at[step, target], recv_sem=rs_recv.at[step, source],
                device_id={"kp": target}, device_id_type=MESH,
            )

        def ag_copy(source, target):
            ref = image.at[step].at[chunk(source)]
            return pltpu.make_async_remote_copy(
                src_ref=ref, dst_ref=ref,
                send_sem=ag_send.at[step, target], recv_sem=ag_recv.at[step, source],
                device_id={"kp": target}, device_id_type=MESH,
            )

        def z_copy(source, target):
            ref = correlations.at[step, source]
            return pltpu.make_async_remote_copy(
                src_ref=ref, dst_ref=ref,
                send_sem=z_send.at[step, target], recv_sem=z_recv.at[step, source],
                device_id={"ka": target}, device_id_type=MESH,
            )

        def far_copy(target):
            return pltpu.make_async_remote_copy(
                src_ref=far_image.at[step], dst_ref=far_image.at[step],
                send_sem=far_send.at[step, target], recv_sem=far_recv.at[step],
                device_id={"ka": target}, device_id_type=MESH,
            )

        def loop(first, count, body):
            def one(d, carry):
                body(d)
                return carry

            lax.fori_loop(first, count, one, 0)

        total = jnp.zeros((vectors, rows), F32)
        for f in range(far):
            far_vectors = far_start[f] if step == 0 else far_bf16[f]
            total += lax.dot_general(
                far_vectors, kernel[:, f * side : (f + 1) * side], NT, preferred_element_type=F32
            )
        product[step] = total
        if step == 0:
            pl.semaphore_wait(barrier, size_ka - 1 + size_kp - 1)
        loop(1, size_kp, lambda d: rs_copy(kp, (kp + d) % size_kp).start())
        received[step, kp] = product[step, own_rows, own_lanes]
        loop(1, size_kp, lambda d: rs_copy((kp + size_kp - d) % size_kp, kp).wait_recv())
        current = start if step == 0 else out
        value = energies[:, own_lanes] * current[own_rows, own_lanes]
        image[step, own_rows, own_lanes] = value + jnp.sum(received[step], axis=0)
        loop(1, size_kp, lambda d: ag_copy(kp, (kp + d) % size_kp).start())
        loop(1, size_kp, lambda d: ag_copy((kp + size_kp - d) % size_kp, kp).wait_recv())
        whole = image[step]
        correlations[step, ka] = lax.dot_general(
            whole, jnp.concatenate([whole, padding], axis=0), NT,
            precision=lax.Precision.HIGHEST, preferred_element_type=F32,
        )
        loop(1, size_ka, lambda d: z_copy(ka, (ka + d) % size_ka).start())
        if step + 1 < STEPS:
            @pl.when(ka == owner)
            def _():
                for f in range(far):
                    far_image[step, f] = image[
                        step, :, pl.ds(pl.multiple_of((offset + f) * side, side), side)
                    ].astype(BF16)
                loop(1, size_ka, lambda d: far_copy((ka + d) % size_ka).start())
        loop(1, size_ka, lambda d: z_copy((ka + size_ka - d) % size_ka, ka).wait_recv())
        correlation = correlations[step, 0]
        for z in range(1, size_ka):
            correlation = correlation + correlations[step, z]
        inverse = inverse_factor(correlation * (1.0 / total_rows))
        out[...] = jnp.dot(
            inverse, jnp.concatenate([padding, whole], axis=0),
            precision=lax.Precision.HIGHEST, preferred_element_type=F32,
        )
        if step + 1 < STEPS:
            @pl.when(ka != owner)
            def _():
                far_copy(ka).wait_recv()

            for f in range(far):
                far_bf16[f] = jnp.dot(
                    inverse,
                    jnp.concatenate([padding[:, :side], far_image[step, f].astype(F32)], axis=0),
                    precision=lax.Precision.HIGHEST, preferred_element_type=F32,
                ).astype(BF16)

            @pl.when(ka == owner)
            def _():
                loop(1, size_ka, lambda d: far_copy((ka + d) % size_ka).wait_send())
        loop(1, size_kp, lambda d: rs_copy(kp, (kp + d) % size_kp).wait_send())
        loop(1, size_kp, lambda d: ag_copy(kp, (kp + d) % size_kp).wait_send())
        loop(1, size_ka, lambda d: z_copy(ka, (ka + d) % size_ka).wait_send())


def subspace(size_ka, size_kp, kernel, far_start, energies, start):
    vectors, rows = start.shape
    far, _, side = far_start.shape
    width = rows // (size_kp // (vectors // 8))
    dma = pltpu.SemaphoreType.DMA
    return pl.pallas_call(
        functools.partial(subspace_kernel, size_ka, size_kp),
        out_shape=jax.ShapeDtypeStruct((vectors, rows), F32),
        in_specs=[VMEM] * 4,
        out_specs=VMEM,
        scratch_shapes=[
            pltpu.VMEM((STEPS, vectors, rows), F32),
            pltpu.VMEM((STEPS, vectors, rows), F32),
            pltpu.VMEM((STEPS, far, vectors, side), BF16),
            pltpu.VMEM((far, vectors, side), BF16),
            pltpu.VMEM((STEPS, size_kp, 8, width), F32),
            pltpu.VMEM((STEPS, size_ka, vectors, 2 * vectors), F32),
            dma((STEPS, size_kp)), dma((STEPS, size_kp)),
            dma((STEPS, size_kp)), dma((STEPS, size_kp)),
            dma((STEPS, size_ka)), dma((STEPS, size_ka)),
            dma((STEPS, size_ka)), dma((STEPS,)),
        ],
        compiler_params=pltpu.CompilerParams(
            collective_id=1, has_side_effects=True, vmem_limit_bytes=32 * 2**20
        ),
    )(kernel, far_start, energies, start)


def transfer_table(near_cells, far_cells, grid_x):
    step_x = (near_cells[:, None] // GRID_Y - far_cells[None, :] // GRID_Y) % grid_x
    step_y = (near_cells[:, None] % GRID_Y - far_cells[None, :] % GRID_Y) % GRID_Y
    return (step_x * GRID_Y + step_y).reshape(-1)


def on_device(band_form, interp_coef, screen, coulomb, shift_map, grid_order, energies, initial):
    size_ka = lax.axis_size("ka")
    size_kp = lax.axis_size("kp")
    near = band_form.shape[0]
    points = near * size_ka
    far = points // size_kp
    side = interp_coef.shape[1]
    near_cells = lax.dynamic_slice_in_dim(grid_order, lax.axis_index("ka") * near, near)
    far_cells = lax.dynamic_slice_in_dim(grid_order, lax.axis_index("kp") * far, far)
    transfers = transfer_table(near_cells, far_cells, points // GRID_Y)
    start = initial.T
    start_points = initial.astype(BF16).reshape(near, side, -1).transpose(0, 2, 1)
    cols = screen.transpose(1, 0, 2).reshape(screen.shape[1], -1)
    coef_t = interp_coef.reshape(near, NV, NC, side).transpose(0, 3, 2, 1).reshape(near, side, side)
    far_form, far_coef, far_start, all_cols = exchange(
        size_ka, size_kp, far, band_form, interp_coef, start_points, cols
    )
    kernel = blocks(
        near, far, screen.shape[2], transfers, band_form, far_form, coef_t, far_coef, all_cols,
        coulomb[None, :], shift_map[:, None, :],
    )
    out = subspace(size_ka, size_kp, kernel, far_start, energies[None, :], start)
    return kernel, out.T


def solution(mesh):
    return jax.shard_map(
        on_device,
        mesh=mesh,
        in_specs=(
            P("ka", None, None),
            P("ka", None, None),
            P("ka", "kp", None),
            P(),
            P(),
            P(),
            P("ka"),
            P("ka", None),
        ),
        out_specs=(P("ka", "kp"), P("ka", None)),
        check_vma=False,
    )
```

```python
import functools

import jax
import jax.numpy as jnp
from jax import lax
from jax.experimental import pallas as pl
from jax.experimental.pallas import tpu as pltpu
from jax.sharding import PartitionSpec as P

NV = 8
NC = 16
STEPS = 2
GRID_Y = 8
LANES = 128
CHUNK = 512
MESH = pl.DeviceIdType.MESH
VMEM = pl.BlockSpec(memory_space=pltpu.VMEM)
SMEM = pl.BlockSpec(memory_space=pltpu.SMEM)
NT = (((1,), (1,)), ((), ()))
TN = (((0,), (0,)), ((), ()))
F32 = jnp.float32
BF16 = jnp.bfloat16


def inverse_factor(matrix):
    size = matrix.shape[0]
    row = lax.broadcasted_iota(jnp.int32, matrix.shape, 0)
    lane = lax.broadcasted_iota(jnp.int32, matrix.shape, 1)
    work = jnp.where(lane == row + size, 1.0, matrix)
    for j in range(size - 1):
        pivot_row = work[j : j + 1, :]
        scaled_row = pivot_row / pivot_row[:, j : j + 1]
        work = work - jnp.where(row > j, work[:, j : j + 1], 0.0) * scaled_row
    diagonal = jnp.sum(jnp.where(lane == row, work, 0.0), axis=1, keepdims=True)
    return jnp.where(lane >= size, work * lax.rsqrt(diagonal), 0.0)


def whole_kernel(
    size_ka, size_kp,
    grid_order, form, coef, screen, coulomb, shift_map, energies, initial,
    kernel, subspace,
    far_form, far_coef, far_start, all_cols, source, conductions, valences, direct, packed, start,
    product, image, far_image, far_bf16, received, correlations,
    up_sem, down_sem, far_sem, z_send, z_recv, plane_send, plane_recv, core_send, core_recv,
    rs_send, rs_recv, ag_send, ag_recv, c_send, c_recv, far_send, far_recv,
):
    ka, kp = lax.axis_index("ka"), lax.axis_index("kp")
    chips = size_kp // 2
    chip, core = kp // 2, kp % 2
    near, far = form.shape[0], far_form.shape[0]
    owner = kp * far // near
    offset = kp * far % near
    per_owner, cut, group = screen.shape
    waves = form.shape[2]
    pieces = waves // LANES
    bands = NV + NC
    side = NV * NC
    pairs = near * far
    grid_x = near * size_ka // GRID_Y

    barrier = pltpu.get_barrier_semaphore()

    def greet_z(d, carry):
        pl.semaphore_signal(barrier, inc=1, device_id={"ka": (ka + d) % size_ka}, device_id_type=MESH)
        return carry

    def greet_plane(d, carry):
        pl.semaphore_signal(barrier, inc=1, device_id={"kp": (kp + d) % size_kp}, device_id_type=MESH)
        return carry

    lax.fori_loop(1, size_ka, greet_z, 0)
    lax.fori_loop(1, size_kp, greet_plane, 0)

    @pl.when(ka == owner)
    def _():
        far_form[...] = form[pl.ds(offset, far)]
        far_coef[...] = coef[pl.ds(offset, far)]
        for f in range(far):
            rows = pl.ds(pl.multiple_of((offset + f) * side, side), side)
            far_start[f] = initial[rows, :].T.astype(BF16)

    def part(z, p):
        return all_cols.at[z, pl.ds(pl.multiple_of(p * cut, cut), cut), :]

    all_cols[ka, pl.ds(pl.multiple_of(kp * cut, cut), cut), :] = jnp.concatenate(
        [screen[n] for n in range(per_owner)], axis=1
    )
    pl.semaphore_wait(barrier, size_ka - 1 + size_kp - 1)

    sent = [far_form.at[i] for i in range(far)] + [far_coef, far_start]

    def far_move(i, sem, target):
        return pltpu.make_async_remote_copy(
            src_ref=sent[i], dst_ref=sent[i], send_sem=sem.at[i], recv_sem=far_sem.at[i],
            device_id={"ka": target}, device_id_type=MESH,
        )

    goes_up = (ka >= owner) & (ka < size_ka - 1)
    goes_down = (ka <= owner) & (ka > 0)
    above, below = (ka + 1) % size_ka, (ka + size_ka - 1) % size_ka

    def z_move(z, target):
        return pltpu.make_async_remote_copy(
            src_ref=part(z, kp), dst_ref=part(z, kp), send_sem=z_send.at[target],
            recv_sem=z_recv.at[z], device_id={"ka": target}, device_id_type=MESH,
        )

    def plane_move(z, c, target):
        ref = part(z, c * 2 + core)
        return pltpu.make_async_remote_copy(
            src_ref=ref, dst_ref=ref, send_sem=plane_send.at[z, target],
            recv_sem=plane_recv.at[z, c],
            device_id={"kp": target * 2 + core}, device_id_type=MESH,
        )

    def core_move(z, c, from_core):
        ref = part(z, c * 2 + from_core)
        return pltpu.make_async_remote_copy(
            src_ref=ref, dst_ref=ref, send_sem=core_send.at[z, c], recv_sem=core_recv.at[z, c],
            device_id={"kp": chip * 2 + 1 - core}, device_id_type=MESH,
        )

    def spread(z):
        def to_plane(d, carry):
            plane_move(z, chip, (chip + d) % chips).start()
            return carry

        lax.fori_loop(1, chips, to_plane, 0)
        core_move(z, chip, core).start()

    def forward(i):
        @pl.when(goes_up)
        def _():
            far_move(i, up_sem, above).start()

        @pl.when(goes_down)
        def _():
            far_move(i, down_sem, below).start()

    @pl.when(ka == owner)
    def _():
        for i in range(len(sent)):
            forward(i)

    def to_z(d, carry):
        z_move(ka, (ka + d) % size_ka).start()
        return carry

    lax.fori_loop(1, size_ka, to_z, 0)
    spread(ka)

    def relay(first, last):
        @pl.when(ka != owner)
        def _():
            for i in range(first, last):
                far_move(i, up_sem, above).wait_recv()
                forward(i)

    relay(0, far)

    def from_z(d, carry):
        z = (ka + size_ka - d) % size_ka
        z_move(z, above).wait_recv()
        spread(z)
        return carry

    def from_plane(d, carry):
        z = (ka + size_ka - d) % size_ka

        def one(e, inner):
            c = (chip + chips - e) % chips
            plane_move(z, c, (chip + e) % chips).wait_recv()
            core_move(z, c, core).start()
            return inner

        return lax.fori_loop(1, chips, one, carry)

    for f in range(far):
        wide = far_form[f].astype(F32)
        source[f] = jnp.concatenate(
            [wide[:, h * LANES : (h + 1) * LANES] for h in range(pieces)], axis=0
        ).astype(BF16)

    def transfer(k, f):
        near_cell = grid_order[ka * near + k]
        far_cell = grid_order[kp * far + f]
        step_x = (near_cell // GRID_Y - far_cell // GRID_Y + grid_x) % grid_x
        step_y = (near_cell % GRID_Y - far_cell % GRID_Y + GRID_Y) % GRID_Y
        return step_x * GRID_Y + step_y

    z_steps = -(-(size_ka - 1) // 2)
    plane_steps = -(-size_ka // 4)
    first_plane = pairs - 5
    square = NV * NV

    def one_pair(n, carry):
        k, f = n // far, n % far
        q = transfer(k, f)
        total = jnp.zeros((square, NC * NC), F32)
        for s in range(0, waves, CHUNK):
            index = shift_map[pl.ds(q, 1), s : s + CHUNK]
            low = index & (LANES - 1)
            high = index // LANES
            one_hot = jnp.where(
                lax.broadcasted_iota(jnp.int32, (LANES, CHUNK), 0) == low, 1.0, 0.0
            ).astype(BF16)
            columns = jnp.dot(source[f], one_hot, preferred_element_type=F32)
            mapped = columns[0:bands]
            for h in range(1, pieces):
                mapped = jnp.where(high == h, columns[h * bands : (h + 1) * bands], mapped)
            near_form = form[k, :, s : s + CHUNK].astype(F32)
            valence = jnp.concatenate(
                [near_form[v : v + 1] * mapped[0:NV] for v in range(NV)], axis=0
            ).astype(BF16)
            conduction = jnp.concatenate(
                [near_form[NV + c : NV + c + 1] * mapped[NV:] for c in range(NC)], axis=0
            ).astype(BF16)
            valences[n, :, s : s + CHUNK] = valence
            conductions[n, :, s : s + CHUNK] = conduction
            scaled = (coulomb[:, s : s + CHUNK] * valence.astype(F32)).astype(BF16)
            total += lax.dot_general(scaled, conduction, NT, preferred_element_type=F32)
        direct[pl.ds(pl.multiple_of(n * square, square), square), :] = total

        @pl.when(n == 0)
        def _():
            relay(far, far + 2)

        @pl.when(n < 2)
        def _():
            low_d = 1 + n * z_steps
            lax.fori_loop(low_d, jnp.minimum(low_d + z_steps, size_ka), from_z, 0)

        @pl.when((n >= first_plane) & (n < first_plane + 4))
        def _():
            low_d = (n - first_plane) * plane_steps
            lax.fori_loop(low_d, jnp.minimum(low_d + plane_steps, size_ka), from_plane, 0)

        return carry

    lax.fori_loop(0, pairs, one_pair, 0)

    def finish(n, carry):
        z, c = n // chips, n % chips
        core_move(z, c, 1 - core).wait_recv()
        core_move(z, c, core).wait_send()
        return carry

    lax.fori_loop(0, size_ka * chips, finish, 0)

    def screening(n, carry):
        q = transfer(n // far, n % far)
        columns = all_cols[q // per_owner]
        left = jnp.dot(conductions[n], columns, preferred_element_type=F32)
        right = jnp.dot(valences[n], columns, preferred_element_type=F32)
        lane = lax.broadcasted_iota(jnp.int32, right.shape, 1)
        right = jnp.where(lane // group == q % per_owner, right, 0.0)
        at = pl.ds(pl.multiple_of(n * square, square), square)
        direct[at, :] += lax.dot_general(
            right, left, NT, precision=lax.Precision.HIGHEST, preferred_element_type=F32
        )
        return carry

    lax.fori_loop(0, pairs, screening, 0)

    all_rows = pairs * square
    row = lax.broadcasted_iota(jnp.int32, (all_rows, LANES), 0)
    lane = lax.broadcasted_iota(jnp.int32, (all_rows, LANES), 1)
    keep = row % NV == lane // NC
    sum_row = lax.broadcasted_iota(jnp.int32, (pairs * NV, all_rows), 0)
    sum_col = lax.broadcasted_iota(jnp.int32, (pairs * NV, all_rows), 1)
    sums = jnp.where(sum_col // NV == sum_row, 1.0, 0.0).astype(BF16)
    pick_row = lax.broadcasted_iota(jnp.int32, (LANES, LANES), 0)
    pick_lane = lax.broadcasted_iota(jnp.int32, (LANES, LANES), 1)
    per_half = LANES // NC
    for c in range(NC):
        pick = jnp.where(
            (pick_row // NC == c % per_half) & (pick_row % NC == pick_lane % NC), 1.0, 0.0
        ).astype(BF16)
        half_at = c // per_half * LANES
        wide = jnp.dot(
            direct[:, half_at : half_at + LANES].astype(BF16), pick, preferred_element_type=F32
        )
        wide = jnp.where(keep, wide, 0.0).astype(BF16)
        packed[pl.ds(c, pairs * NV, stride=NC), :] = jnp.dot(
            sums, wide, preferred_element_type=F32
        )
    for k in range(near):
        for f in range(far):
            at = (k * far + f) * side
            block = packed[at : at + side, :].astype(BF16)
            half = jnp.dot(block, far_coef[f], preferred_element_type=F32).astype(BF16)
            kernel[k * side : (k + 1) * side, f * side : (f + 1) * side] = lax.dot_general(
                coef[k], half, TN, preferred_element_type=F32
            ).astype(BF16)

    start[...] = initial[...].T
    vectors, rows = start.shape
    row_groups = vectors // 8
    lane_groups = size_kp // row_groups
    width = rows // lane_groups
    total_rows = rows * size_ka

    def chunk(p):
        return (
            pl.ds(pl.multiple_of(p // lane_groups * 8, 8), 8),
            pl.ds(pl.multiple_of(p % lane_groups * width, width), width),
        )

    own_rows, own_lanes = chunk(kp)
    padding = jnp.zeros((vectors, rows), F32)

    for step in range(STEPS):
        def rs_move(source, target):
            return pltpu.make_async_remote_copy(
                src_ref=product.at[step].at[chunk(target)],
                dst_ref=received.at[step, source],
                send_sem=rs_send.at[step, target], recv_sem=rs_recv.at[step, source],
                device_id={"kp": target}, device_id_type=MESH,
            )

        def ag_move(source, target):
            ref = image.at[step].at[chunk(source)]
            return pltpu.make_async_remote_copy(
                src_ref=ref, dst_ref=ref,
                send_sem=ag_send.at[step, target], recv_sem=ag_recv.at[step, source],
                device_id={"kp": target}, device_id_type=MESH,
            )

        def c_move(source, target):
            ref = correlations.at[step, source]
            return pltpu.make_async_remote_copy(
                src_ref=ref, dst_ref=ref,
                send_sem=c_send.at[step, target], recv_sem=c_recv.at[step, source],
                device_id={"ka": target}, device_id_type=MESH,
            )

        def image_move(target):
            return pltpu.make_async_remote_copy(
                src_ref=far_image.at[step], dst_ref=far_image.at[step],
                send_sem=far_send.at[step, target], recv_sem=far_recv.at[step],
                device_id={"ka": target}, device_id_type=MESH,
            )

        def loop(first, count, body):
            def one(d, carry):
                body(d)
                return carry

            lax.fori_loop(first, count, one, 0)

        total = jnp.zeros((vectors, rows), F32)
        for f in range(far):
            far_vectors = far_start[f] if step == 0 else far_bf16[f]
            total += lax.dot_general(
                far_vectors, kernel[:, f * side : (f + 1) * side], NT, preferred_element_type=F32
            )
        product[step] = total
        loop(1, size_kp, lambda d: rs_move(kp, (kp + d) % size_kp).start())
        received[step, kp] = product[step, own_rows, own_lanes]
        loop(1, size_kp, lambda d: rs_move((kp + size_kp - d) % size_kp, kp).wait_recv())
        value = energies[:, own_lanes] * start[own_rows, own_lanes]
        image[step, own_rows, own_lanes] = value + jnp.sum(received[step], axis=0)
        loop(1, size_kp, lambda d: ag_move(kp, (kp + d) % size_kp).start())
        loop(1, size_kp, lambda d: ag_move((kp + size_kp - d) % size_kp, kp).wait_recv())
        whole = image[step]
        correlations[step, ka] = lax.dot_general(
            whole, jnp.concatenate([whole, padding], axis=0), NT,
            precision=lax.Precision.HIGHEST, preferred_element_type=F32,
        )
        loop(1, size_ka, lambda d: c_move(ka, (ka + d) % size_ka).start())
        if step + 1 < STEPS:
            @pl.when(ka == owner)
            def _():
                for f in range(far):
                    far_image[step, f] = image[
                        step, :, pl.ds(pl.multiple_of((offset + f) * side, side), side)
                    ].astype(BF16)
                loop(1, size_ka, lambda d: image_move((ka + d) % size_ka).start())
        loop(1, size_ka, lambda d: c_move((ka + size_ka - d) % size_ka, ka).wait_recv())
        correlation = correlations[step, 0]
        for z in range(1, size_ka):
            correlation = correlation + correlations[step, z]
        inverse = inverse_factor(correlation * (1.0 / total_rows))
        start[...] = jnp.dot(
            inverse, jnp.concatenate([padding, whole], axis=0),
            precision=lax.Precision.HIGHEST, preferred_element_type=F32,
        )
        if step + 1 < STEPS:
            @pl.when(ka != owner)
            def _():
                image_move(ka).wait_recv()

            for f in range(far):
                far_bf16[f] = jnp.dot(
                    inverse,
                    jnp.concatenate([padding[:, :side], far_image[step, f].astype(F32)], axis=0),
                    precision=lax.Precision.HIGHEST, preferred_element_type=F32,
                ).astype(BF16)

            @pl.when(ka == owner)
            def _():
                loop(1, size_ka, lambda d: image_move((ka + d) % size_ka).wait_send())
        loop(1, size_kp, lambda d: rs_move(kp, (kp + d) % size_kp).wait_send())
        loop(1, size_kp, lambda d: ag_move(kp, (kp + d) % size_kp).wait_send())
        loop(1, size_ka, lambda d: c_move(ka, (ka + d) % size_ka).wait_send())

    subspace[...] = start[...].T

    def finish_plane(n, carry):
        z, e = n // (chips - 1), n % (chips - 1) + 1
        plane_move(z, chip, (chip + e) % chips).wait_send()
        return carry

    lax.fori_loop(0, size_ka * (chips - 1), finish_plane, 0)

    def finish_z(d, carry):
        z_move(ka, (ka + d) % size_ka).wait_send()
        return carry

    lax.fori_loop(1, size_ka, finish_z, 0)
    for i in range(len(sent)):
        @pl.when(goes_up)
        def _():
            far_move(i, up_sem, above).wait_send()

        @pl.when(goes_down)
        def _():
            far_move(i, down_sem, below).wait_send()


def on_device(band_form, interp_coef, screen, coulomb, shift_map, grid_order, energies, initial):
    size_ka = lax.axis_size("ka")
    size_kp = lax.axis_size("kp")
    near, bands, waves = band_form.shape
    side = interp_coef.shape[1]
    rows, vectors = initial.shape
    per_owner, _, group = screen.shape
    far = near * size_ka // size_kp
    pairs = near * far
    chips = size_kp // 2
    width = rows // (size_kp // (vectors // 8))
    dma = pltpu.SemaphoreType.DMA
    return pl.pallas_call(
        functools.partial(whole_kernel, size_ka, size_kp),
        out_shape=(
            jax.ShapeDtypeStruct((rows, far * side), BF16),
            jax.ShapeDtypeStruct((rows, vectors), F32),
        ),
        in_specs=[SMEM] + [VMEM] * 7,
        out_specs=(VMEM, VMEM),
        scratch_shapes=[
            pltpu.VMEM((far, bands, waves), BF16),
            pltpu.VMEM((far, side, side), BF16),
            pltpu.VMEM((far, vectors, side), BF16),
            pltpu.VMEM((size_ka, waves, per_owner * group), BF16),
            pltpu.VMEM((far, waves // LANES * bands, LANES), BF16),
            pltpu.VMEM((pairs, NC * NC, waves), BF16),
            pltpu.VMEM((pairs, NV * NV, waves), BF16),
            pltpu.VMEM((pairs * NV * NV, NC * NC), F32),
            pltpu.VMEM((pairs * side, LANES), F32),
            pltpu.VMEM((vectors, rows), F32),
            pltpu.VMEM((STEPS, vectors, rows), F32),
            pltpu.VMEM((STEPS, vectors, rows), F32),
            pltpu.VMEM((STEPS, far, vectors, side), BF16),
            pltpu.VMEM((far, vectors, side), BF16),
            pltpu.VMEM((STEPS, size_kp, 8, width), F32),
            pltpu.VMEM((STEPS, size_ka, vectors, 2 * vectors), F32),
            dma((far + 2,)), dma((far + 2,)), dma((far + 2,)),
            dma((size_ka,)), dma((size_ka,)),
            dma((size_ka, chips)), dma((size_ka, chips)),
            dma((size_ka, chips)), dma((size_ka, chips)),
            dma((STEPS, size_kp)), dma((STEPS, size_kp)),
            dma((STEPS, size_kp)), dma((STEPS, size_kp)),
            dma((STEPS, size_ka)), dma((STEPS, size_ka)),
            dma((STEPS, size_ka)), dma((STEPS,)),
        ],
        compiler_params=pltpu.CompilerParams(
            collective_id=0, has_side_effects=True, vmem_limit_bytes=56 * 2**20
        ),
    )(
        grid_order, band_form, interp_coef, screen, coulomb[None, :], shift_map,
        energies[None, :], initial,
    )


def solution(mesh):
    return jax.shard_map(
        on_device,
        mesh=mesh,
        in_specs=(
            P("ka", None, None),
            P("ka", None, None),
            P("ka", "kp", None),
            P(),
            P(),
            P(),
            P("ka"),
            P("ka", None),
        ),
        out_specs=(P("ka", "kp"), P("ka", None)),
        check_vma=False,
    )
```

```python
import functools

import jax
import jax.numpy as jnp
from jax import lax
from jax.experimental import pallas as pl
from jax.experimental.pallas import tpu as pltpu
from jax.sharding import PartitionSpec as P

NV = 8
NC = 16
STEPS = 2
GRID_Y = 8
LANES = 128
DEPTH = 256
CHUNK = 512
SUB = 16
MESH = pl.DeviceIdType.MESH
VMEM = pl.BlockSpec(memory_space=pltpu.VMEM)
SMEM = pl.BlockSpec(memory_space=pltpu.SMEM)
NT = (((1,), (1,)), ((), ()))
TN = (((0,), (0,)), ((), ()))
F32 = jnp.float32
BF16 = jnp.bfloat16


def inverse_factor(matrix):
    size = matrix.shape[0]
    row = lax.broadcasted_iota(jnp.int32, matrix.shape, 0)
    lane = lax.broadcasted_iota(jnp.int32, matrix.shape, 1)
    work = jnp.where(lane == row + size, 1.0, matrix)
    for j in range(0, size, 2):
        first, second = work[j : j + 1, :], work[j + 1 : j + 2, :]
        first_inverse = 1.0 / first[:, j : j + 1]
        ratio = second[:, j : j + 1] * first_inverse
        second = second - ratio * first
        second_scaled = second * (1.0 / second[:, j + 1 : j + 2])
        first_scaled = first * first_inverse - ratio * second_scaled
        update = work[:, j : j + 1] * first_scaled + work[:, j + 1 : j + 2] * second_scaled
        work = jnp.where(row > j + 1, work - update, jnp.where(row == j + 1, second, work))
    diagonal = jnp.sum(jnp.where(lane == row, work, 0.0), axis=1, keepdims=True)
    return jnp.where(lane >= size, work * lax.rsqrt(diagonal), 0.0)


def whole_kernel(
    size_ka, size_kp,
    grid_order, form, coef, screen, coulomb, shift_map, energies, initial,
    kernel, subspace,
    far_form, far_coef, far_start, all_cols, source, near_rows, conductions, valences, direct, packed, start,
    product, image, far_image, far_bf16, received, correlations,
    up_sem, down_sem, far_sem, z_send, z_recv, plane_send, plane_recv, core_send, core_recv,
    rs_send, rs_recv, ag_send, ag_recv, c_send, c_recv, far_send, far_recv,
):
    ka, kp = lax.axis_index("ka"), lax.axis_index("kp")
    chips = size_kp // 2
    chip, core = kp // 2, kp % 2
    near, far = form.shape[0], far_form.shape[0]
    owner = kp * far // near
    offset = kp * far % near
    per_owner, group, cut = screen.shape
    waves = form.shape[2]
    pieces = waves // DEPTH
    bands = NV + NC
    side = NV * NC
    pairs = near * far
    grid_x = near * size_ka // GRID_Y

    barrier = pltpu.get_barrier_semaphore()

    def greet_z(d, carry):
        pl.semaphore_signal(barrier, inc=1, device_id={"ka": (ka + d) % size_ka}, device_id_type=MESH)
        return carry

    def greet_plane(d, carry):
        pl.semaphore_signal(barrier, inc=1, device_id={"kp": (kp + d) % size_kp}, device_id_type=MESH)
        return carry

    lax.fori_loop(1, size_ka, greet_z, 0)
    lax.fori_loop(1, size_kp, greet_plane, 0)

    @pl.when(ka == owner)
    def _():
        far_form[...] = form[pl.ds(offset, far)]
        far_coef[...] = coef[pl.ds(offset, far)]
        for f in range(far):
            far_start[f] = initial[
                :, pl.ds(pl.multiple_of((offset + f) * side, side), side)
            ].astype(BF16)

    def part(z, p):
        return all_cols.at[z, pl.ds(pl.multiple_of(p * cut, cut), cut), :]

    all_cols[ka, pl.ds(pl.multiple_of(kp * cut, cut), cut), :] = (
        screen[...].reshape(per_owner * group, cut).astype(F32).T.astype(BF16)
    )
    pl.semaphore_wait(barrier, size_ka - 1 + size_kp - 1)

    half_waves = waves // 2
    sent = [
        far_form.at[f, :, h * half_waves : (h + 1) * half_waves]
        for f in range(far)
        for h in range(2)
    ] + [far_coef, far_start]
    forms = 2 * far

    def far_move(i, sem, target):
        return pltpu.make_async_remote_copy(
            src_ref=sent[i], dst_ref=sent[i], send_sem=sem.at[i], recv_sem=far_sem.at[i],
            device_id={"ka": target}, device_id_type=MESH,
        )

    goes_up = (ka >= owner) & (ka < size_ka - 1)
    goes_down = (ka <= owner) & (ka > 0)
    above, below = (ka + 1) % size_ka, (ka + size_ka - 1) % size_ka

    def z_move(z, target):
        return pltpu.make_async_remote_copy(
            src_ref=part(z, kp), dst_ref=part(z, kp), send_sem=z_send.at[target],
            recv_sem=z_recv.at[z], device_id={"ka": target}, device_id_type=MESH,
        )

    def plane_move(z, c, target):
        ref = part(z, c * 2 + core)
        return pltpu.make_async_remote_copy(
            src_ref=ref, dst_ref=ref, send_sem=plane_send.at[z, target],
            recv_sem=plane_recv.at[z, c],
            device_id={"kp": target * 2 + core}, device_id_type=MESH,
        )

    def core_move(z, c, from_core):
        ref = part(z, c * 2 + from_core)
        return pltpu.make_async_remote_copy(
            src_ref=ref, dst_ref=ref, send_sem=core_send.at[z, c], recv_sem=core_recv.at[z, c],
            device_id={"kp": chip * 2 + 1 - core}, device_id_type=MESH,
        )

    def spread(z):
        def to_plane(d, carry):
            plane_move(z, chip, (chip + d) % chips).start()
            return carry

        lax.fori_loop(1, chips, to_plane, 0)
        core_move(z, chip, core).start()

    def forward(i):
        @pl.when(goes_up)
        def _():
            far_move(i, up_sem, above).start()

        @pl.when(goes_down)
        def _():
            far_move(i, down_sem, below).start()

    @pl.when(ka == owner)
    def _():
        for i in range(len(sent)):
            forward(i)

    spread(ka)

    def spread_near(k, carry):
        wide = form[k].astype(F32)
        for v in range(0, NV, 2):
            near_rows[k, v // 2] = jnp.concatenate(
                [jnp.broadcast_to(wide[v + i : v + i + 1], (NV, waves)) for i in range(2)], axis=0
            ).astype(BF16)
        for c in range(NC):
            near_rows[k, NV // 2 + c] = jnp.broadcast_to(
                wide[NV + c : NV + c + 1], (NC, waves)
            ).astype(BF16)
        return carry

    lax.fori_loop(0, near, spread_near, 0)

    def relay(first, last):
        @pl.when(ka != owner)
        def _():
            for i in range(first, last):
                far_move(i, up_sem, above).wait_recv()
                forward(i)

    relay(0, forms)

    def to_z(d, carry):
        z_move(ka, (ka + d) % size_ka).start()
        return carry

    lax.fori_loop(1, size_ka, to_z, 0)

    def from_z(d, carry):
        z = (ka + size_ka - d) % size_ka
        z_move(z, above).wait_recv()
        spread(z)
        return carry

    def from_plane(d, carry):
        z = (ka + size_ka - d) % size_ka

        def one(e, inner):
            c = (chip + chips - e) % chips
            plane_move(z, c, (chip + e) % chips).wait_recv()
            core_move(z, c, core).start()
            return inner

        return lax.fori_loop(1, chips, one, carry)

    for f in range(far):
        wide = far_form[f].astype(F32)
        source[f] = jnp.concatenate(
            [wide[:, h * DEPTH : (h + 1) * DEPTH] for h in range(pieces)], axis=0
        ).astype(BF16)

    def transfer(k, f):
        near_cell = grid_order[ka * near + k]
        far_cell = grid_order[kp * far + f]
        step_x = (near_cell // GRID_Y - far_cell // GRID_Y + grid_x) % grid_x
        step_y = (near_cell % GRID_Y - far_cell % GRID_Y + GRID_Y) % GRID_Y
        return step_x * GRID_Y + step_y

    z_steps = -(-(size_ka - 1) // 2)
    plane_steps = -(-size_ka // 4)
    first_plane = pairs - 5
    square = NV * NV

    steps = lax.broadcasted_iota(jnp.int32, (SUB, CHUNK), 0)
    one, zero = jnp.ones((SUB, CHUNK), BF16), jnp.zeros((SUB, CHUNK), BF16)

    def one_pair(n, carry):
        k, f = n // far, n % far
        q = transfer(k, f)
        total = jnp.zeros((square, NC * NC), F32)
        for s in range(0, waves, CHUNK):
            index = shift_map[pl.ds(q, 1), s : s + CHUNK]
            low = jnp.broadcast_to(index % DEPTH, (SUB, CHUNK)).astype(F32).astype(BF16)
            high = index // DEPTH
            one_hot = jnp.concatenate(
                [
                    jnp.where((steps + r).astype(F32).astype(BF16) == low, one, zero)
                    for r in range(0, DEPTH, SUB)
                ],
                axis=0,
            )
            columns = jnp.dot(source[f], one_hot, preferred_element_type=F32)
            mapped = columns[0:bands]
            for h in range(1, pieces):
                mapped = jnp.where(high == h, columns[h * bands : (h + 1) * bands], mapped)
            top = mapped[0:NV]
            top = jnp.concatenate([top, top], axis=0).astype(BF16)
            rest = mapped[NV:].astype(BF16)
            valence = jnp.concatenate(
                [near_rows[k, i, :, s : s + CHUNK] * top for i in range(NV // 2)], axis=0
            )
            conduction = jnp.concatenate(
                [near_rows[k, NV // 2 + c, :, s : s + CHUNK] * rest for c in range(NC)], axis=0
            )
            valences[n, :, s : s + CHUNK] = valence
            conductions[n, :, s : s + CHUNK] = conduction
            scaled = (coulomb[:, s : s + CHUNK] * valence.astype(F32)).astype(BF16)
            total += lax.dot_general(scaled, conduction, NT, preferred_element_type=F32)
        direct[pl.ds(pl.multiple_of(n * square, square), square), :] = total

        @pl.when(n == 0)
        def _():
            relay(forms, forms + 2)

        @pl.when(n < 2)
        def _():
            low_d = 1 + n * z_steps
            lax.fori_loop(low_d, jnp.minimum(low_d + z_steps, size_ka), from_z, 0)

        @pl.when((n >= first_plane) & (n < first_plane + 4))
        def _():
            low_d = (n - first_plane) * plane_steps
            lax.fori_loop(low_d, jnp.minimum(low_d + plane_steps, size_ka), from_plane, 0)

        return carry

    lax.fori_loop(0, pairs, one_pair, 0)

    def finish(n, carry):
        z, c = n // chips, n % chips
        core_move(z, c, 1 - core).wait_recv()
        core_move(z, c, core).wait_send()
        return carry

    lax.fori_loop(0, size_ka * chips, finish, 0)

    def screening(k, carry):
        for f in range(far):
            n = k * far + f
            q = transfer(k, f)
            columns = all_cols[q // per_owner]
            left = jnp.dot(conductions[n], columns, preferred_element_type=F32)
            right = jnp.dot(valences[n], columns, preferred_element_type=F32)
            lane = lax.broadcasted_iota(jnp.int32, right.shape, 1)
            right = jnp.where(lane // group == q % per_owner, right, 0.0)
            at = pl.ds(pl.multiple_of(n * square, square), square)
            direct[at, :] += lax.dot_general(
                right.astype(BF16), left.astype(BF16), NT, preferred_element_type=F32
            )
        return carry

    lax.fori_loop(0, near, screening, 0)

    all_rows = pairs * square
    row = lax.broadcasted_iota(jnp.int32, (all_rows, LANES), 0)
    lane = lax.broadcasted_iota(jnp.int32, (all_rows, LANES), 1)
    keep = row % NV == lane // NC
    sum_row = lax.broadcasted_iota(jnp.int32, (pairs * NV, all_rows), 0)
    sum_col = lax.broadcasted_iota(jnp.int32, (pairs * NV, all_rows), 1)
    sums = jnp.where(sum_col // NV == sum_row, 1.0, 0.0).astype(BF16)
    pick_row = lax.broadcasted_iota(jnp.int32, (LANES, LANES), 0)
    pick_lane = lax.broadcasted_iota(jnp.int32, (LANES, LANES), 1)
    per_half = LANES // NC
    for c in range(NC):
        pick = jnp.where(
            (pick_row // NC == c % per_half) & (pick_row % NC == pick_lane % NC), 1.0, 0.0
        ).astype(BF16)
        half_at = c // per_half * LANES
        wide = jnp.dot(
            direct[:, half_at : half_at + LANES].astype(BF16), pick, preferred_element_type=F32
        )
        wide = jnp.where(keep, wide, 0.0).astype(BF16)
        packed[pl.ds(c, pairs * NV, stride=NC), :] = jnp.dot(
            sums, wide, preferred_element_type=F32
        )
    for k in range(near):
        for f in range(far):
            at = (k * far + f) * side
            block = packed[at : at + side, :].astype(BF16)
            half = jnp.dot(block, far_coef[f], preferred_element_type=F32).astype(BF16)
            kernel[k * side : (k + 1) * side, f * side : (f + 1) * side] = lax.dot_general(
                coef[k], half, TN, preferred_element_type=F32
            ).astype(BF16)

    start[...] = initial[...]
    vectors, rows = start.shape
    row_groups = vectors // 8
    lane_groups = size_kp // row_groups
    width = rows // lane_groups
    total_rows = rows * size_ka

    def chunk(p):
        return (
            pl.ds(pl.multiple_of(p // lane_groups * 8, 8), 8),
            pl.ds(pl.multiple_of(p % lane_groups * width, width), width),
        )

    own_rows, own_lanes = chunk(kp)
    padding = jnp.zeros((vectors, rows), F32)

    for step in range(STEPS):
        def rs_move(source, target):
            return pltpu.make_async_remote_copy(
                src_ref=product.at[step].at[chunk(target)],
                dst_ref=received.at[step, source],
                send_sem=rs_send.at[step, target], recv_sem=rs_recv.at[step, source],
                device_id={"kp": target}, device_id_type=MESH,
            )

        def ag_move(source, target):
            ref = image.at[step].at[chunk(source)]
            return pltpu.make_async_remote_copy(
                src_ref=ref, dst_ref=ref,
                send_sem=ag_send.at[step, target], recv_sem=ag_recv.at[step, source],
                device_id={"kp": target}, device_id_type=MESH,
            )

        def c_move(source, target):
            ref = correlations.at[step, source]
            return pltpu.make_async_remote_copy(
                src_ref=ref, dst_ref=ref,
                send_sem=c_send.at[step, target], recv_sem=c_recv.at[step, source],
                device_id={"ka": target}, device_id_type=MESH,
            )

        def image_move(target):
            return pltpu.make_async_remote_copy(
                src_ref=far_image.at[step], dst_ref=far_image.at[step],
                send_sem=far_send.at[step, target], recv_sem=far_recv.at[step],
                device_id={"ka": target}, device_id_type=MESH,
            )

        def loop(first, count, body):
            def one(d, carry):
                body(d)
                return carry

            lax.fori_loop(first, count, one, 0)

        total = jnp.zeros((vectors, rows), F32)
        for f in range(far):
            far_vectors = far_start[f] if step == 0 else far_bf16[f]
            total += lax.dot_general(
                far_vectors, kernel[:, f * side : (f + 1) * side], NT, preferred_element_type=F32
            )
        product[step] = total
        loop(1, size_kp, lambda d: rs_move(kp, (kp + d) % size_kp).start())
        received[step, kp] = product[step, own_rows, own_lanes]
        loop(1, size_kp, lambda d: rs_move((kp + size_kp - d) % size_kp, kp).wait_recv())
        value = energies[:, own_lanes] * start[own_rows, own_lanes]
        image[step, own_rows, own_lanes] = value + jnp.sum(received[step], axis=0)
        loop(1, size_kp, lambda d: ag_move(kp, (kp + d) % size_kp).start())
        loop(1, size_kp, lambda d: ag_move((kp + size_kp - d) % size_kp, kp).wait_recv())
        whole = image[step]
        correlations[step, ka] = lax.dot_general(
            whole, jnp.concatenate([whole, padding], axis=0), NT,
            precision=lax.Precision.HIGHEST, preferred_element_type=F32,
        )
        loop(1, size_ka, lambda d: c_move(ka, (ka + d) % size_ka).start())
        if step + 1 < STEPS:
            @pl.when(ka == owner)
            def _():
                for f in range(far):
                    far_image[step, f] = image[
                        step, :, pl.ds(pl.multiple_of((offset + f) * side, side), side)
                    ].astype(BF16)
                loop(1, size_ka, lambda d: image_move((ka + d) % size_ka).start())
        loop(1, size_ka, lambda d: c_move((ka + size_ka - d) % size_ka, ka).wait_recv())
        correlation = correlations[step, 0]
        for z in range(1, size_ka):
            correlation = correlation + correlations[step, z]
        inverse = inverse_factor(correlation * (1.0 / total_rows))
        start[...] = jnp.dot(
            inverse, jnp.concatenate([padding, whole], axis=0),
            precision=lax.Precision.HIGHEST, preferred_element_type=F32,
        )
        if step + 1 < STEPS:
            @pl.when(ka != owner)
            def _():
                image_move(ka).wait_recv()

            for f in range(far):
                far_bf16[f] = jnp.dot(
                    inverse,
                    jnp.concatenate([padding[:, :side], far_image[step, f].astype(F32)], axis=0),
                    precision=lax.Precision.HIGHEST, preferred_element_type=F32,
                ).astype(BF16)

            @pl.when(ka == owner)
            def _():
                loop(1, size_ka, lambda d: image_move((ka + d) % size_ka).wait_send())
        loop(1, size_kp, lambda d: rs_move(kp, (kp + d) % size_kp).wait_send())
        loop(1, size_kp, lambda d: ag_move(kp, (kp + d) % size_kp).wait_send())
        loop(1, size_ka, lambda d: c_move(ka, (ka + d) % size_ka).wait_send())

    subspace[...] = start[...]

    def finish_plane(n, carry):
        z, e = n // (chips - 1), n % (chips - 1) + 1
        plane_move(z, chip, (chip + e) % chips).wait_send()
        return carry

    lax.fori_loop(0, size_ka * (chips - 1), finish_plane, 0)

    def finish_z(d, carry):
        z_move(ka, (ka + d) % size_ka).wait_send()
        return carry

    lax.fori_loop(1, size_ka, finish_z, 0)
    for i in range(len(sent)):
        @pl.when(goes_up)
        def _():
            far_move(i, up_sem, above).wait_send()

        @pl.when(goes_down)
        def _():
            far_move(i, down_sem, below).wait_send()


def on_device(band_form, interp_coef, screen, coulomb, shift_map, grid_order, energies, initial):
    size_ka = lax.axis_size("ka")
    size_kp = lax.axis_size("kp")
    near, bands, waves = band_form.shape
    side = interp_coef.shape[1]
    rows, vectors = initial.shape
    per_owner, _, group = screen.shape
    far = near * size_ka // size_kp
    pairs = near * far
    chips = size_kp // 2
    width = rows // (size_kp // (vectors // 8))
    dma = pltpu.SemaphoreType.DMA
    kernel, subspace = pl.pallas_call(
        functools.partial(whole_kernel, size_ka, size_kp),
        out_shape=(
            jax.ShapeDtypeStruct((rows, far * side), BF16),
            jax.ShapeDtypeStruct((vectors, rows), F32),
        ),
        in_specs=[SMEM] + [VMEM] * 7,
        out_specs=(VMEM, VMEM),
        scratch_shapes=[
            pltpu.VMEM((far, bands, waves), BF16),
            pltpu.VMEM((far, side, side), BF16),
            pltpu.VMEM((far, vectors, side), BF16),
            pltpu.VMEM((size_ka, waves, per_owner * group), BF16),
            pltpu.VMEM((far, waves // DEPTH * bands, DEPTH), BF16),
            pltpu.VMEM((near, NV // 2 + NC, SUB, waves), BF16),
            pltpu.VMEM((pairs, NC * NC, waves), BF16),
            pltpu.VMEM((pairs, NV * NV, waves), BF16),
            pltpu.VMEM((pairs * NV * NV, NC * NC), F32),
            pltpu.VMEM((pairs * side, LANES), F32),
            pltpu.VMEM((vectors, rows), F32),
            pltpu.VMEM((STEPS, vectors, rows), F32),
            pltpu.VMEM((STEPS, vectors, rows), F32),
            pltpu.VMEM((STEPS, far, vectors, side), BF16),
            pltpu.VMEM((far, vectors, side), BF16),
            pltpu.VMEM((STEPS, size_kp, 8, width), F32),
            pltpu.VMEM((STEPS, size_ka, vectors, 2 * vectors), F32),
            dma((2 * far + 2,)), dma((2 * far + 2,)), dma((2 * far + 2,)),
            dma((size_ka,)), dma((size_ka,)),
            dma((size_ka, chips)), dma((size_ka, chips)),
            dma((size_ka, chips)), dma((size_ka, chips)),
            dma((STEPS, size_kp)), dma((STEPS, size_kp)),
            dma((STEPS, size_kp)), dma((STEPS, size_kp)),
            dma((STEPS, size_ka)), dma((STEPS, size_ka)),
            dma((STEPS, size_ka)), dma((STEPS,)),
        ],
        compiler_params=pltpu.CompilerParams(
            collective_id=0, has_side_effects=True, vmem_limit_bytes=56 * 2**20
        ),
    )(
        grid_order, band_form, interp_coef, screen.transpose(0, 2, 1), coulomb[None, :], shift_map,
        energies[None, :], initial.T,
    )
    return kernel, subspace.T


def solution(mesh):
    return jax.shard_map(
        on_device,
        mesh=mesh,
        in_specs=(
            P("ka", None, None),
            P("ka", None, None),
            P("ka", "kp", None),
            P(),
            P(),
            P(),
            P("ka"),
            P("ka", None),
        ),
        out_specs=(P("ka", "kp"), P("ka", None)),
        check_vma=False,
    )
```

```python
import functools

import jax
import jax.numpy as jnp
from jax import lax
from jax.experimental import pallas as pl
from jax.experimental.pallas import tpu as pltpu
from jax.sharding import PartitionSpec as P

NV = 8
NC = 16
STEPS = 2
GRID_Y = 8
LANES = 128
DEPTH = 256
CHUNK = 512
SUB = 16
COPIES = 4
MESH = pl.DeviceIdType.MESH
VMEM = pl.BlockSpec(memory_space=pltpu.VMEM)
SMEM = pl.BlockSpec(memory_space=pltpu.SMEM)
NT = (((1,), (1,)), ((), ()))
TN = (((0,), (0,)), ((), ()))
F32 = jnp.float32
BF16 = jnp.bfloat16


def log2(size):
    return size.bit_length() - 1


def inverse_factor(matrix):
    size = matrix.shape[0]
    work = jnp.concatenate([matrix, jnp.zeros_like(matrix)], axis=1)
    row = lax.broadcasted_iota(jnp.int32, work.shape, 0)
    lane = lax.broadcasted_iota(jnp.int32, work.shape, 1)
    work = jnp.where(lane == row + size, 1.0, work)
    for j in range(0, size, 2):
        first, second = work[j : j + 1, :], work[j + 1 : j + 2, :]
        first_inverse = 1.0 / first[:, j : j + 1]
        ratio = second[:, j : j + 1] * first_inverse
        second = second - ratio * first
        second_scaled = second * (1.0 / second[:, j + 1 : j + 2])
        first_scaled = first * first_inverse - ratio * second_scaled
        update = work[:, j : j + 1] * first_scaled + work[:, j + 1 : j + 2] * second_scaled
        work = jnp.where(row > j + 1, work - update, jnp.where(row == j + 1, second, work))
    diagonal = jnp.sum(jnp.where(lane == row, work, 0.0), axis=1, keepdims=True)
    return jnp.where(lane >= size, work * lax.rsqrt(diagonal), 0.0)


def whole_kernel(
    size_ka, size_kp,
    grid_order, form, coef, screen, coulomb, shift_map, energies, initial,
    kernel, subspace,
    far_form, far_coef, far_start, all_cols, source, near_rows, conductions, valences, direct, packed, inverse_rows,
    product, image, far_image, far_bf16, received, correlations,
    up_sem, down_sem, far_sem, z_send, z_recv, plane_send, plane_recv, core_send, core_recv,
    rs_send, rs_recv, ag_send, ag_recv, c_send, c_recv, far_send, far_recv,
):
    ka, kp = lax.axis_index("ka"), lax.axis_index("kp")
    chips = size_kp // 2
    chip, core = kp // 2, kp % 2
    near, far = form.shape[0], far_form.shape[0]
    owner = kp * far // near
    offset = kp * far % near
    per_owner, group, cut = screen.shape
    waves = form.shape[2]
    pieces = waves // DEPTH
    bands = NV + NC
    side = NV * NC
    pairs = near * far
    grid_x = near * size_ka // GRID_Y

    barrier = pltpu.get_barrier_semaphore()

    def greet_z(d, carry):
        pl.semaphore_signal(barrier, inc=1, device_id={"ka": (ka + d) % size_ka}, device_id_type=MESH)
        return carry

    def greet_plane(d, carry):
        pl.semaphore_signal(barrier, inc=1, device_id={"kp": (kp + d) % size_kp}, device_id_type=MESH)
        return carry

    lax.fori_loop(1, size_ka, greet_z, 0)
    lax.fori_loop(1, size_kp, greet_plane, 0)

    @pl.when(ka == owner)
    def _():
        far_form[...] = form[pl.ds(offset, far)]
        far_coef[...] = coef[pl.ds(offset, far)]
        for f in range(far):
            far_start[f] = initial[
                :, pl.ds(pl.multiple_of((offset + f) * side, side), side)
            ].astype(BF16)

    def part(z, p):
        return all_cols.at[z, pl.ds(pl.multiple_of(p * cut, cut), cut), :]

    all_cols[ka, pl.ds(pl.multiple_of(kp * cut, cut), cut), :] = (
        screen[...].reshape(per_owner * group, cut).astype(F32).T.astype(BF16)
    )
    pl.semaphore_wait(barrier, size_ka - 1 + size_kp - 1)

    half_waves = waves // 2
    sent = [
        far_form.at[f, :, h * half_waves : (h + 1) * half_waves]
        for f in range(far)
        for h in range(2)
    ] + [far_coef, far_start]
    forms = 2 * far

    def far_move(i, sem, target):
        return pltpu.make_async_remote_copy(
            src_ref=sent[i], dst_ref=sent[i], send_sem=sem.at[i], recv_sem=far_sem.at[i],
            device_id={"ka": target}, device_id_type=MESH,
        )

    goes_up = (ka >= owner) & (ka < size_ka - 1)
    goes_down = (ka <= owner) & (ka > 0)
    above, below = (ka + 1) % size_ka, (ka + size_ka - 1) % size_ka

    def z_move(z, target):
        return pltpu.make_async_remote_copy(
            src_ref=part(z, kp), dst_ref=part(z, kp), send_sem=z_send.at[target],
            recv_sem=z_recv.at[z], device_id={"ka": target}, device_id_type=MESH,
        )

    def plane_move(z, c, target):
        ref = part(z, c * 2 + core)
        return pltpu.make_async_remote_copy(
            src_ref=ref, dst_ref=ref, send_sem=plane_send.at[z, target],
            recv_sem=plane_recv.at[z, c],
            device_id={"kp": target * 2 + core}, device_id_type=MESH,
        )

    def core_move(z, c, from_core):
        ref = part(z, c * 2 + from_core)
        return pltpu.make_async_remote_copy(
            src_ref=ref, dst_ref=ref, send_sem=core_send.at[z, c], recv_sem=core_recv.at[z, c],
            device_id={"kp": chip * 2 + 1 - core}, device_id_type=MESH,
        )

    def spread(z):
        def to_plane(d, carry):
            plane_move(z, chip, (chip + d) % chips).start()
            return carry

        lax.fori_loop(1, chips, to_plane, 0)
        core_move(z, chip, core).start()

    def forward(i):
        @pl.when(goes_up)
        def _():
            far_move(i, up_sem, above).start()

        @pl.when(goes_down)
        def _():
            far_move(i, down_sem, below).start()

    @pl.when(ka == owner)
    def _():
        for i in range(len(sent)):
            forward(i)

    spread(ka)

    def spread_near(k, carry):
        wide = form[k].astype(F32)
        for v in range(0, NV, 2):
            near_rows[k, v // 2] = jnp.concatenate(
                [jnp.broadcast_to(wide[v + i : v + i + 1], (NV, waves)) for i in range(2)], axis=0
            ).astype(BF16)
        for c in range(NC):
            near_rows[k, NV // 2 + c] = jnp.broadcast_to(
                wide[NV + c : NV + c + 1], (NC, waves)
            ).astype(BF16)
        return carry

    lax.fori_loop(0, near, spread_near, 0)

    def relay(first, last):
        @pl.when(ka != owner)
        def _():
            for i in range(first, last):
                far_move(i, up_sem, above).wait_recv()
                forward(i)

    relay(0, 2)

    def to_z(d, carry):
        z_move(ka, (ka + d) % size_ka).start()
        return carry

    lax.fori_loop(1, size_ka, to_z, 0)

    def from_z(d, carry):
        z = (ka + size_ka - d) % size_ka
        z_move(z, above).wait_recv()
        spread(z)
        return carry

    def from_plane(d, carry):
        z = (ka + size_ka - d) % size_ka

        def one(e, inner):
            c = (chip + chips - e) % chips
            plane_move(z, c, (chip + e) % chips).wait_recv()
            core_move(z, c, core).start()
            return inner

        return lax.fori_loop(1, chips, one, carry)

    def stack(f):
        wide = far_form[f].astype(F32)
        source[f] = jnp.concatenate(
            [wide[:, h * DEPTH : (h + 1) * DEPTH] for h in range(pieces)], axis=0
        ).astype(BF16)

    stack(0)

    def transfer(k, f):
        near_cell = grid_order[ka * near + k]
        far_cell = grid_order[kp * far + f]
        step_x = (near_cell // GRID_Y - far_cell // GRID_Y + grid_x) % grid_x
        step_y = (near_cell % GRID_Y - far_cell % GRID_Y + GRID_Y) % GRID_Y
        return step_x * GRID_Y + step_y

    z_steps = -(-(size_ka - 1) // 2)
    plane_steps = -(-size_ka // 4)
    first_plane = pairs - 5
    square = NV * NV

    steps = lax.broadcasted_iota(jnp.int32, (SUB, CHUNK), 0)
    one, zero = jnp.ones((SUB, CHUNK), BF16), jnp.zeros((SUB, CHUNK), BF16)

    def one_pair(n, carry):
        f, k = n // near, n % near
        slot = k * far + f
        q = transfer(k, f)
        total = jnp.zeros((square, NC * NC), F32)
        for s in range(0, waves, CHUNK):
            index = shift_map[pl.ds(q, 1), s : s + CHUNK]
            low = jnp.broadcast_to(index & (DEPTH - 1), (SUB, CHUNK)).astype(F32).astype(BF16)
            high = index >> log2(DEPTH)
            one_hot = jnp.concatenate(
                [
                    jnp.where((steps + r).astype(F32).astype(BF16) == low, one, zero)
                    for r in range(0, DEPTH, SUB)
                ],
                axis=0,
            )
            columns = jnp.dot(source[f], one_hot, preferred_element_type=F32)
            mapped = columns[0:bands]
            for h in range(1, pieces):
                mapped = jnp.where(high == h, columns[h * bands : (h + 1) * bands], mapped)
            top = mapped[0:NV]
            top = jnp.concatenate([top, top], axis=0).astype(BF16)
            rest = mapped[NV:].astype(BF16)
            valence = jnp.concatenate(
                [near_rows[k, i, :, s : s + CHUNK] * top for i in range(NV // 2)], axis=0
            )
            conduction = jnp.concatenate(
                [near_rows[k, NV // 2 + c, :, s : s + CHUNK] * rest for c in range(NC)], axis=0
            )
            valences[slot, :, s : s + CHUNK] = valence
            conductions[slot, :, s : s + CHUNK] = conduction
            scaled = (coulomb[:, s : s + CHUNK] * valence.astype(F32)).astype(BF16)
            total += lax.dot_general(scaled, conduction, NT, preferred_element_type=F32)
        direct[pl.ds(pl.multiple_of(slot * square, square), square), :] = total

        for after in range(1, far):
            @pl.when(n == after - 1)
            def _():
                relay(2 * after, 2 * after + 2)
                stack(after)

        @pl.when(n == far - 1)
        def _():
            relay(forms, forms + 2)

        @pl.when((n >= 1) & (n < 3))
        def _():
            low_d = 1 + (n - 1) * z_steps
            lax.fori_loop(low_d, jnp.minimum(low_d + z_steps, size_ka), from_z, 0)

        @pl.when((n >= first_plane) & (n < first_plane + 4))
        def _():
            low_d = (n - first_plane) * plane_steps
            lax.fori_loop(low_d, jnp.minimum(low_d + plane_steps, size_ka), from_plane, 0)

        return carry

    lax.fori_loop(0, pairs, one_pair, 0)

    def finish(n, carry):
        z, c = n // chips, n % chips
        core_move(z, c, 1 - core).wait_recv()
        core_move(z, c, core).wait_send()
        return carry

    lax.fori_loop(0, size_ka * chips, finish, 0)

    def screening(k, carry):
        for f in range(far):
            n = k * far + f
            q = transfer(k, f)
            columns = all_cols[q // per_owner]
            left = jnp.dot(conductions[n], columns, preferred_element_type=F32)
            right = jnp.dot(valences[n], columns, preferred_element_type=F32)
            lane = lax.broadcasted_iota(jnp.int32, right.shape, 1)
            right = jnp.where((lane >> log2(group)) == q % per_owner, right, 0.0)
            at = pl.ds(pl.multiple_of(n * square, square), square)
            direct[at, :] += lax.dot_general(
                right.astype(BF16), left.astype(BF16), NT, preferred_element_type=F32
            )
        return carry

    lax.fori_loop(0, near, screening, 0)

    all_rows = pairs * square
    row = lax.broadcasted_iota(jnp.int32, (all_rows, LANES), 0)
    lane = lax.broadcasted_iota(jnp.int32, (all_rows, LANES), 1)
    keep = (row & (NV - 1)) == (lane >> log2(NC))
    sum_row = lax.broadcasted_iota(jnp.int32, (pairs * NV, all_rows), 0)
    sum_col = lax.broadcasted_iota(jnp.int32, (pairs * NV, all_rows), 1)
    sums = jnp.where((sum_col >> log2(NV)) == sum_row, 1.0, 0.0).astype(BF16)
    pick_row = lax.broadcasted_iota(jnp.int32, (LANES, LANES), 0)
    pick_lane = lax.broadcasted_iota(jnp.int32, (LANES, LANES), 1)
    per_half = LANES // NC
    same = (pick_row & (NC - 1)) == (pick_lane & (NC - 1))
    for c in range(NC):
        pick = jnp.where(
            ((pick_row >> log2(NC)) == c % per_half) & same, 1.0, 0.0
        ).astype(BF16)
        half_at = c // per_half * LANES
        wide = jnp.dot(
            direct[:, half_at : half_at + LANES].astype(BF16), pick, preferred_element_type=F32
        )
        wide = jnp.where(keep, wide, 0.0).astype(BF16)
        packed[pl.ds(c, pairs * NV, stride=NC), :] = jnp.dot(
            sums, wide, preferred_element_type=F32
        )
    for k in range(near):
        for f in range(far):
            at = (k * far + f) * side
            block = packed[at : at + side, :].astype(BF16)
            half = jnp.dot(block, far_coef[f], preferred_element_type=F32).astype(BF16)
            kernel[k * side : (k + 1) * side, f * side : (f + 1) * side] = lax.dot_general(
                coef[k], half, TN, preferred_element_type=F32
            ).astype(BF16)

    vectors, rows = initial.shape
    half = vectors // 2
    row_groups = vectors // 8
    lane_groups = size_kp // row_groups
    width = rows // lane_groups
    total_rows = rows * size_ka

    def chunk(p):
        return (
            pl.ds(pl.multiple_of(p // lane_groups * 8, 8), 8),
            pl.ds(pl.multiple_of(p % lane_groups * width, width), width),
        )

    own_rows, own_lanes = chunk(kp)
    padding = jnp.zeros((vectors, rows), F32)

    for step in range(STEPS):
        def rs_move(source, target):
            return pltpu.make_async_remote_copy(
                src_ref=product.at[step].at[chunk(target)],
                dst_ref=received.at[step, source],
                send_sem=rs_send.at[step, target], recv_sem=rs_recv.at[step, source],
                device_id={"kp": target}, device_id_type=MESH,
            )

        def ag_move(source, target):
            ref = image.at[step].at[chunk(source)]
            return pltpu.make_async_remote_copy(
                src_ref=ref, dst_ref=ref,
                send_sem=ag_send.at[step, target], recv_sem=ag_recv.at[step, source],
                device_id={"kp": target}, device_id_type=MESH,
            )

        def c_move(source, target):
            ref = correlations.at[step, source]
            return pltpu.make_async_remote_copy(
                src_ref=ref, dst_ref=ref,
                send_sem=c_send.at[step, target], recv_sem=c_recv.at[step, source],
                device_id={"ka": target}, device_id_type=MESH,
            )

        def image_move(target):
            return pltpu.make_async_remote_copy(
                src_ref=far_image.at[step], dst_ref=far_image.at[step],
                send_sem=far_send.at[step, target], recv_sem=far_recv.at[step],
                device_id={"ka": target}, device_id_type=MESH,
            )

        def loop(first, count, body):
            def one(d, carry):
                body(d)
                return carry

            lax.fori_loop(first, count, one, 0)

        total = jnp.zeros((vectors, rows), F32)
        for f in range(far):
            far_vectors = far_start[f] if step == 0 else far_bf16[f]
            total += lax.dot_general(
                far_vectors, kernel[:, f * side : (f + 1) * side], NT, preferred_element_type=F32
            )
        product[step] = total
        loop(1, size_kp, lambda d: rs_move(kp, (kp + d) % size_kp).start())
        received[step, kp] = product[step, own_rows, own_lanes]
        if step == 0:
            current = initial[own_rows, own_lanes]
        else:
            current = jnp.dot(
                inverse_rows[own_rows, :],
                jnp.concatenate(
                    [padding[:, :width], image[step - 1, :, own_lanes]], axis=0
                ),
                precision=lax.Precision.HIGHEST, preferred_element_type=F32,
            )
        loop(1, size_kp, lambda d: rs_move((kp + size_kp - d) % size_kp, kp).wait_recv())
        value = energies[:, own_lanes] * current
        image[step, own_rows, own_lanes] = value + jnp.sum(received[step], axis=0)
        loop(1, size_kp, lambda d: ag_move(kp, (kp + d) % size_kp).start())
        loop(1, size_kp, lambda d: ag_move((kp + size_kp - d) % size_kp, kp).wait_recv())
        whole = image[step]
        local = lax.dot_general(
            whole, whole, NT, precision=lax.Precision.HIGHEST, preferred_element_type=F32
        )
        correlations[step, ka] = jnp.concatenate([local[:half], local[half:]], axis=1)
        loop(1, size_ka, lambda d: c_move(ka, (ka + d) % size_ka).start())
        if step + 1 < STEPS:
            @pl.when(ka == owner)
            def _():
                for f in range(far):
                    far_image[step, f] = image[
                        step, :, pl.ds(pl.multiple_of((offset + f) * side, side), side)
                    ]
                loop(1, size_ka, lambda d: image_move((ka + d) % size_ka).start())
        loop(1, size_ka, lambda d: c_move((ka + size_ka - d) % size_ka, ka).wait_recv())
        correlation = correlations[step, 0]
        for z in range(1, size_ka):
            correlation = correlation + correlations[step, z]
        correlation = jnp.concatenate([correlation[:, :vectors], correlation[:, vectors:]], axis=0)
        inverse = inverse_factor(correlation * (1.0 / total_rows))
        if step + 1 < STEPS:
            inverse_rows[...] = inverse
        else:
            subspace[...] = jnp.dot(
                inverse, jnp.concatenate([padding, whole], axis=0),
                precision=lax.Precision.HIGHEST, preferred_element_type=F32,
            )
        if step + 1 < STEPS:
            @pl.when(ka != owner)
            def _():
                image_move(ka).wait_recv()

            for f in range(far):
                far_bf16[f] = jnp.dot(
                    inverse,
                    jnp.concatenate([padding[:, :side], far_image[step, f]], axis=0),
                    precision=lax.Precision.HIGHEST, preferred_element_type=F32,
                ).astype(BF16)

            @pl.when(ka == owner)
            def _():
                loop(1, size_ka, lambda d: image_move((ka + d) % size_ka).wait_send())
        loop(1, size_kp, lambda d: rs_move(kp, (kp + d) % size_kp).wait_send())
        loop(1, size_kp, lambda d: ag_move(kp, (kp + d) % size_kp).wait_send())
        loop(1, size_ka, lambda d: c_move(ka, (ka + d) % size_ka).wait_send())

    def finish_plane(n, carry):
        z, e = n // (chips - 1), n % (chips - 1) + 1
        plane_move(z, chip, (chip + e) % chips).wait_send()
        return carry

    lax.fori_loop(0, size_ka * (chips - 1), finish_plane, 0)

    def finish_z(d, carry):
        z_move(ka, (ka + d) % size_ka).wait_send()
        return carry

    lax.fori_loop(1, size_ka, finish_z, 0)
    for i in range(len(sent)):
        @pl.when(goes_up)
        def _():
            far_move(i, up_sem, above).wait_send()

        @pl.when(goes_down)
        def _():
            far_move(i, down_sem, below).wait_send()


def hand_over_kernel(kernel, subspace, kernel_out, subspace_out, sems):
    rows = kernel.shape[0] // COPIES
    moves = [
        pltpu.make_async_copy(
            kernel.at[pl.ds(i * rows, rows)], kernel_out.at[pl.ds(i * rows, rows)], sems.at[i]
        )
        for i in range(COPIES)
    ] + [pltpu.make_async_copy(subspace, subspace_out, sems.at[COPIES])]
    for move in moves:
        move.start()
    for move in moves:
        move.wait()


def hand_over(kernel, subspace):
    anywhere = pl.BlockSpec(memory_space=pl.ANY)
    return pl.pallas_call(
        hand_over_kernel,
        out_shape=tuple(jax.ShapeDtypeStruct(x.shape, x.dtype) for x in (kernel, subspace)),
        in_specs=[anywhere, anywhere],
        out_specs=(anywhere, anywhere),
        scratch_shapes=[pltpu.SemaphoreType.DMA((COPIES + 1,))],
    )(kernel, subspace)


def on_device(band_form, interp_coef, screen, coulomb, shift_map, grid_order, energies, initial):
    size_ka = lax.axis_size("ka")
    size_kp = lax.axis_size("kp")
    near, bands, waves = band_form.shape
    side = interp_coef.shape[1]
    rows, vectors = initial.shape
    per_owner, _, group = screen.shape
    far = near * size_ka // size_kp
    pairs = near * far
    chips = size_kp // 2
    width = rows // (size_kp // (vectors // 8))
    dma = pltpu.SemaphoreType.DMA
    kernel, subspace = pl.pallas_call(
        functools.partial(whole_kernel, size_ka, size_kp),
        out_shape=(
            jax.ShapeDtypeStruct((rows, far * side), BF16),
            jax.ShapeDtypeStruct((vectors, rows), F32),
        ),
        in_specs=[SMEM] + [VMEM] * 7,
        out_specs=(VMEM, VMEM),
        scratch_shapes=[
            pltpu.VMEM((far, bands, waves), BF16),
            pltpu.VMEM((far, side, side), BF16),
            pltpu.VMEM((far, vectors, side), BF16),
            pltpu.VMEM((size_ka, waves, per_owner * group), BF16),
            pltpu.VMEM((far, waves // DEPTH * bands, DEPTH), BF16),
            pltpu.VMEM((near, NV // 2 + NC, SUB, waves), BF16),
            pltpu.VMEM((pairs, NC * NC, waves), BF16),
            pltpu.VMEM((pairs, NV * NV, waves), BF16),
            pltpu.VMEM((pairs * NV * NV, NC * NC), F32),
            pltpu.VMEM((pairs * side, LANES), F32),
            pltpu.VMEM((vectors, 2 * vectors), F32),
            pltpu.VMEM((STEPS, vectors, rows), F32),
            pltpu.VMEM((STEPS, vectors, rows), F32),
            pltpu.VMEM((STEPS, far, vectors, side), F32),
            pltpu.VMEM((far, vectors, side), BF16),
            pltpu.VMEM((STEPS, size_kp, 8, width), F32),
            pltpu.VMEM((STEPS, size_ka, vectors // 2, 2 * vectors), F32),
            dma((2 * far + 2,)), dma((2 * far + 2,)), dma((2 * far + 2,)),
            dma((size_ka,)), dma((size_ka,)),
            dma((size_ka, chips)), dma((size_ka, chips)),
            dma((size_ka, chips)), dma((size_ka, chips)),
            dma((STEPS, size_kp)), dma((STEPS, size_kp)),
            dma((STEPS, size_kp)), dma((STEPS, size_kp)),
            dma((STEPS, size_ka)), dma((STEPS, size_ka)),
            dma((STEPS, size_ka)), dma((STEPS,)),
        ],
        compiler_params=pltpu.CompilerParams(
            collective_id=0, has_side_effects=True, vmem_limit_bytes=56 * 2**20
        ),
    )(
        grid_order, band_form, interp_coef, screen.transpose(0, 2, 1), coulomb[None, :], shift_map,
        energies[None, :], initial.T,
    )
    kernel, subspace = hand_over(kernel, subspace)
    return kernel, subspace.T


def solution(mesh):
    return jax.shard_map(
        on_device,
        mesh=mesh,
        in_specs=(
            P("ka", None, None),
            P("ka", None, None),
            P("ka", "kp", None),
            P(),
            P(),
            P(),
            P("ka"),
            P("ka", None),
        ),
        out_specs=(P("ka", "kp"), P("ka", None)),
        check_vma=False,
    )
```

```python
import functools

import jax
import jax.numpy as jnp
from jax import lax
from jax.experimental import pallas as pl
from jax.experimental.pallas import tpu as pltpu
from jax.sharding import PartitionSpec as P

NV = 8
NC = 16
STEPS = 2
GRID_Y = 8
LANES = 128
DEPTH = 256
CHUNK = 512
SUB = 16
MESH = pl.DeviceIdType.MESH
VMEM = pl.BlockSpec(memory_space=pltpu.VMEM)
SMEM = pl.BlockSpec(memory_space=pltpu.SMEM)
NT = (((1,), (1,)), ((), ()))
TN = (((0,), (0,)), ((), ()))
F32 = jnp.float32
BF16 = jnp.bfloat16


def log2(size):
    return size.bit_length() - 1


def inverse_factor(matrix):
    size = matrix.shape[0]
    work = jnp.concatenate([matrix, jnp.zeros_like(matrix)], axis=1)
    row = lax.broadcasted_iota(jnp.int32, work.shape, 0)
    lane = lax.broadcasted_iota(jnp.int32, work.shape, 1)
    work = jnp.where(lane == row + size, 1.0, work)
    for j in range(0, size, 2):
        first, second = work[j : j + 1, :], work[j + 1 : j + 2, :]
        first_inverse = 1.0 / first[:, j : j + 1]
        ratio = second[:, j : j + 1] * first_inverse
        second = second - ratio * first
        second_scaled = second * (1.0 / second[:, j + 1 : j + 2])
        first_scaled = first * first_inverse - ratio * second_scaled
        update = work[:, j : j + 1] * first_scaled + work[:, j + 1 : j + 2] * second_scaled
        work = jnp.where(row > j + 1, work - update, jnp.where(row == j + 1, second, work))
    diagonal = jnp.sum(jnp.where(lane == row, work, 0.0), axis=1, keepdims=True)
    return jnp.where(lane >= size, work * lax.rsqrt(diagonal), 0.0)


def whole_kernel(
    size_ka, size_kp,
    grid_order, form, coef, screen, coulomb, shift_map, energies, initial,
    kernel, subspace,
    far_form, far_coef, far_start, all_cols, source, near_rows, conductions, valences, direct, packed, inverse_rows,
    product, image, far_image, far_bf16, received, correlations,
    up_sem, down_sem, far_sem, z_send, z_recv, plane_send, plane_recv, core_send, core_recv,
    rs_send, rs_recv, ag_send, ag_recv, c_send, c_recv, far_send, far_recv,
):
    ka, kp = lax.axis_index("ka"), lax.axis_index("kp")
    chips = size_kp // 2
    chip, core = kp // 2, kp % 2
    near, far = form.shape[0], far_form.shape[0]
    owner = kp * far // near
    offset = kp * far % near
    per_owner, group, cut = screen.shape
    waves = form.shape[2]
    pieces = waves // DEPTH
    bands = NV + NC
    side = NV * NC
    pairs = near * far
    grid_x = near * size_ka // GRID_Y

    barrier = pltpu.get_barrier_semaphore()

    def greet_z(d, carry):
        pl.semaphore_signal(barrier, inc=1, device_id={"ka": (ka + d) % size_ka}, device_id_type=MESH)
        return carry

    def greet_plane(d, carry):
        pl.semaphore_signal(barrier, inc=1, device_id={"kp": (kp + d) % size_kp}, device_id_type=MESH)
        return carry

    lax.fori_loop(1, size_ka, greet_z, 0)
    lax.fori_loop(1, size_kp, greet_plane, 0)

    @pl.when(ka == owner)
    def _():
        far_form[...] = form[pl.ds(offset, far)]
        far_coef[...] = coef[pl.ds(offset, far)]
        for f in range(far):
            far_start[f] = initial[
                :, pl.ds(pl.multiple_of((offset + f) * side, side), side)
            ].astype(BF16)

    def part(z, p):
        return all_cols.at[z, pl.ds(pl.multiple_of(p * cut, cut), cut), :]

    all_cols[ka, pl.ds(pl.multiple_of(kp * cut, cut), cut), :] = (
        screen[...].reshape(per_owner * group, cut).astype(F32).T.astype(BF16)
    )
    pl.semaphore_wait(barrier, size_ka - 1 + size_kp - 1)

    half_waves = waves // 2
    sent = [
        far_form.at[f, :, h * half_waves : (h + 1) * half_waves]
        for f in range(far)
        for h in range(2)
    ] + [far_coef, far_start]
    forms = 2 * far

    def far_move(i, sem, target):
        return pltpu.make_async_remote_copy(
            src_ref=sent[i], dst_ref=sent[i], send_sem=sem.at[i], recv_sem=far_sem.at[i],
            device_id={"ka": target}, device_id_type=MESH,
        )

    goes_up = (ka >= owner) & (ka < size_ka - 1)
    goes_down = (ka <= owner) & (ka > 0)
    above, below = (ka + 1) % size_ka, (ka + size_ka - 1) % size_ka

    def z_move(z, target):
        return pltpu.make_async_remote_copy(
            src_ref=part(z, kp), dst_ref=part(z, kp), send_sem=z_send.at[target],
            recv_sem=z_recv.at[z], device_id={"ka": target}, device_id_type=MESH,
        )

    def plane_move(z, c, target):
        ref = part(z, c * 2 + core)
        return pltpu.make_async_remote_copy(
            src_ref=ref, dst_ref=ref, send_sem=plane_send.at[z, target],
            recv_sem=plane_recv.at[z, c],
            device_id={"kp": target * 2 + core}, device_id_type=MESH,
        )

    def core_move(z, c, from_core):
        ref = part(z, c * 2 + from_core)
        return pltpu.make_async_remote_copy(
            src_ref=ref, dst_ref=ref, send_sem=core_send.at[z, c], recv_sem=core_recv.at[z, c],
            device_id={"kp": chip * 2 + 1 - core}, device_id_type=MESH,
        )

    def spread(z):
        def to_plane(d, carry):
            plane_move(z, chip, (chip + d) % chips).start()
            return carry

        lax.fori_loop(1, chips, to_plane, 0)
        core_move(z, chip, core).start()

    def forward(i):
        @pl.when(goes_up)
        def _():
            far_move(i, up_sem, above).start()

        @pl.when(goes_down)
        def _():
            far_move(i, down_sem, below).start()

    @pl.when(ka == owner)
    def _():
        for i in range(forms):
            forward(i)

    def to_z(d, carry):
        z_move(ka, (ka + d) % size_ka).start()
        return carry

    lax.fori_loop(1, size_ka, to_z, 0)

    spread(ka)

    def spread_near(k, carry):
        wide = form[k].astype(F32)
        for v in range(0, NV, 2):
            near_rows[k, v // 2] = jnp.concatenate(
                [jnp.broadcast_to(wide[v + i : v + i + 1], (NV, waves)) for i in range(2)], axis=0
            ).astype(BF16)
        for c in range(NC):
            near_rows[k, NV // 2 + c] = jnp.broadcast_to(
                wide[NV + c : NV + c + 1], (NC, waves)
            ).astype(BF16)
        return carry

    lax.fori_loop(0, near, spread_near, 0)

    def relay(first, last):
        @pl.when(ka != owner)
        def _():
            for i in range(first, last):
                far_move(i, up_sem, above).wait_recv()
                forward(i)

    relay(0, 2)

    def from_z(d, carry):
        z = (ka + size_ka - d) % size_ka
        z_move(z, above).wait_recv()
        spread(z)
        return carry

    def from_plane(d, carry):
        z = (ka + size_ka - d) % size_ka

        def one(e, inner):
            c = (chip + chips - e) % chips
            plane_move(z, c, (chip + e) % chips).wait_recv()
            core_move(z, c, core).start()
            return inner

        return lax.fori_loop(1, chips, one, carry)

    def stack(f):
        wide = far_form[f].astype(F32)
        source[f] = jnp.concatenate(
            [wide[:, h * DEPTH : (h + 1) * DEPTH] for h in range(pieces)], axis=0
        ).astype(BF16)

    stack(0)
    lax.fori_loop(1, size_ka, from_z, 0)

    def transfer(k, f):
        near_cell = grid_order[ka * near + k]
        far_cell = grid_order[kp * far + f]
        step_x = (near_cell // GRID_Y - far_cell // GRID_Y + grid_x) % grid_x
        step_y = (near_cell % GRID_Y - far_cell % GRID_Y + GRID_Y) % GRID_Y
        return step_x * GRID_Y + step_y

    plane_steps = -(-size_ka // 4)
    first_plane = pairs - 6
    square = NV * NV

    steps = lax.broadcasted_iota(jnp.int32, (SUB, CHUNK), 0)
    one, zero = jnp.ones((SUB, CHUNK), BF16), jnp.zeros((SUB, CHUNK), BF16)

    def one_pair(n, carry):
        f, k = n // near, n % near
        slot = k * far + f
        q = transfer(k, f)
        total = jnp.zeros((square, NC * NC), F32)
        for s in range(0, waves, CHUNK):
            index = shift_map[pl.ds(q, 1), s : s + CHUNK]
            low = jnp.broadcast_to(index & (DEPTH - 1), (SUB, CHUNK)).astype(F32).astype(BF16)
            high = index >> log2(DEPTH)
            one_hot = jnp.concatenate(
                [
                    jnp.where((steps + r).astype(F32).astype(BF16) == low, one, zero)
                    for r in range(0, DEPTH, SUB)
                ],
                axis=0,
            )
            columns = jnp.dot(source[f], one_hot, preferred_element_type=F32)
            mapped = columns[0:bands]
            for h in range(1, pieces):
                mapped = jnp.where(high == h, columns[h * bands : (h + 1) * bands], mapped)
            top = mapped[0:NV]
            top = jnp.concatenate([top, top], axis=0).astype(BF16)
            rest = mapped[NV:].astype(BF16)
            valence = jnp.concatenate(
                [near_rows[k, i, :, s : s + CHUNK] * top for i in range(NV // 2)], axis=0
            )
            conduction = jnp.concatenate(
                [near_rows[k, NV // 2 + c, :, s : s + CHUNK] * rest for c in range(NC)], axis=0
            )
            valences[slot, :, s : s + CHUNK] = valence
            conductions[slot, :, s : s + CHUNK] = conduction
            scaled = (coulomb[:, s : s + CHUNK] * valence.astype(F32)).astype(BF16)
            total += lax.dot_general(scaled, conduction, NT, preferred_element_type=F32)
        direct[pl.ds(pl.multiple_of(slot * square, square), square), :] = total

        for after in range(1, far):
            @pl.when(n == after - 1)
            def _():
                relay(2 * after, 2 * after + 2)
                stack(after)

        @pl.when(n == far - 1)
        def _():
            @pl.when(ka == owner)
            def _():
                for i in range(forms, forms + 2):
                    forward(i)

            relay(forms, forms + 2)

        @pl.when((n >= first_plane) & (n < first_plane + 4))
        def _():
            low_d = (n - first_plane) * plane_steps
            lax.fori_loop(low_d, jnp.minimum(low_d + plane_steps, size_ka), from_plane, 0)

        return carry

    lax.fori_loop(0, pairs, one_pair, 0)

    def finish(n, carry):
        z, c = n // chips, n % chips
        core_move(z, c, 1 - core).wait_recv()
        core_move(z, c, core).wait_send()
        return carry

    lax.fori_loop(0, size_ka * chips, finish, 0)

    def screening(k, carry):
        for f in range(far):
            n = k * far + f
            q = transfer(k, f)
            columns = all_cols[q // per_owner]
            left = jnp.dot(conductions[n], columns, preferred_element_type=F32)
            right = jnp.dot(valences[n], columns, preferred_element_type=F32)
            lane = lax.broadcasted_iota(jnp.int32, right.shape, 1)
            right = jnp.where((lane >> log2(group)) == q % per_owner, right, 0.0)
            at = pl.ds(pl.multiple_of(n * square, square), square)
            direct[at, :] += lax.dot_general(
                right.astype(BF16), left.astype(BF16), NT, preferred_element_type=F32
            )
        return carry

    lax.fori_loop(0, near, screening, 0)

    all_rows = pairs * square
    row = lax.broadcasted_iota(jnp.int32, (all_rows, LANES), 0)
    lane = lax.broadcasted_iota(jnp.int32, (all_rows, LANES), 1)
    keep = (row & (NV - 1)) == (lane >> log2(NC))
    sum_row = lax.broadcasted_iota(jnp.int32, (pairs * NV, all_rows), 0)
    sum_col = lax.broadcasted_iota(jnp.int32, (pairs * NV, all_rows), 1)
    sums = jnp.where((sum_col >> log2(NV)) == sum_row, 1.0, 0.0).astype(BF16)
    pick_row = lax.broadcasted_iota(jnp.int32, (LANES, LANES), 0)
    pick_lane = lax.broadcasted_iota(jnp.int32, (LANES, LANES), 1)
    per_half = LANES // NC
    same = (pick_row & (NC - 1)) == (pick_lane & (NC - 1))
    for c in range(NC):
        pick = jnp.where(
            ((pick_row >> log2(NC)) == c % per_half) & same, 1.0, 0.0
        ).astype(BF16)
        half_at = c // per_half * LANES
        wide = jnp.dot(
            direct[:, half_at : half_at + LANES].astype(BF16), pick, preferred_element_type=F32
        )
        wide = jnp.where(keep, wide, 0.0).astype(BF16)
        packed[pl.ds(c, pairs * NV, stride=NC), :] = jnp.dot(
            sums, wide, preferred_element_type=F32
        )
    for k in range(near):
        for f in range(far):
            at = (k * far + f) * side
            block = packed[at : at + side, :].astype(BF16)
            half = jnp.dot(block, far_coef[f], preferred_element_type=F32).astype(BF16)
            kernel[k * side : (k + 1) * side, f * side : (f + 1) * side] = lax.dot_general(
                coef[k], half, TN, preferred_element_type=F32
            ).astype(BF16)

    vectors, rows = initial.shape
    half = vectors // 2
    row_groups = vectors // 8
    lane_groups = size_kp // row_groups
    width = rows // lane_groups
    total_rows = rows * size_ka

    def chunk(p):
        return (
            pl.ds(pl.multiple_of(p // lane_groups * 8, 8), 8),
            pl.ds(pl.multiple_of(p % lane_groups * width, width), width),
        )

    own_rows, own_lanes = chunk(kp)
    padding = jnp.zeros((vectors, rows), F32)

    for step in range(STEPS):
        def rs_move(source, target):
            return pltpu.make_async_remote_copy(
                src_ref=product.at[step].at[chunk(target)],
                dst_ref=received.at[step, source],
                send_sem=rs_send.at[step, target], recv_sem=rs_recv.at[step, source],
                device_id={"kp": target}, device_id_type=MESH,
            )

        def ag_move(source, target):
            ref = image.at[step].at[chunk(source)]
            return pltpu.make_async_remote_copy(
                src_ref=ref, dst_ref=ref,
                send_sem=ag_send.at[step, target], recv_sem=ag_recv.at[step, source],
                device_id={"kp": target}, device_id_type=MESH,
            )

        def c_move(source, target):
            ref = correlations.at[step, source]
            return pltpu.make_async_remote_copy(
                src_ref=ref, dst_ref=ref,
                send_sem=c_send.at[step, target], recv_sem=c_recv.at[step, source],
                device_id={"ka": target}, device_id_type=MESH,
            )

        def image_move(target):
            return pltpu.make_async_remote_copy(
                src_ref=far_image.at[step], dst_ref=far_image.at[step],
                send_sem=far_send.at[step, target], recv_sem=far_recv.at[step],
                device_id={"ka": target}, device_id_type=MESH,
            )

        def loop(first, count, body):
            def one(d, carry):
                body(d)
                return carry

            lax.fori_loop(first, count, one, 0)

        total = jnp.zeros((vectors, rows), F32)
        for f in range(far):
            far_vectors = far_start[f] if step == 0 else far_bf16[f]
            total += lax.dot_general(
                far_vectors, kernel[:, f * side : (f + 1) * side], NT, preferred_element_type=F32
            )
        product[step] = total
        loop(1, size_kp, lambda d: rs_move(kp, (kp + d) % size_kp).start())
        received[step, kp] = product[step, own_rows, own_lanes]
        if step == 0:
            current = initial[own_rows, own_lanes]
        else:
            current = jnp.dot(
                inverse_rows[own_rows, :],
                jnp.concatenate(
                    [padding[:, :width], image[step - 1, :, own_lanes]], axis=0
                ),
                precision=lax.Precision.HIGHEST, preferred_element_type=F32,
            )
        loop(1, size_kp, lambda d: rs_move((kp + size_kp - d) % size_kp, kp).wait_recv())
        value = energies[:, own_lanes] * current
        image[step, own_rows, own_lanes] = value + jnp.sum(received[step], axis=0)
        loop(1, size_kp, lambda d: ag_move(kp, (kp + d) % size_kp).start())
        loop(1, size_kp, lambda d: ag_move((kp + size_kp - d) % size_kp, kp).wait_recv())
        whole = image[step]
        local = lax.dot_general(
            whole, whole, NT, precision=lax.Precision.HIGHEST, preferred_element_type=F32
        )
        correlations[step, ka] = jnp.concatenate([local[:half], local[half:]], axis=1)
        loop(1, size_ka, lambda d: c_move(ka, (ka + d) % size_ka).start())
        if step + 1 < STEPS:
            @pl.when(ka == owner)
            def _():
                for f in range(far):
                    far_image[step, f] = image[
                        step, :, pl.ds(pl.multiple_of((offset + f) * side, side), side)
                    ]
                loop(1, size_ka, lambda d: image_move((ka + d) % size_ka).start())
        loop(1, size_ka, lambda d: c_move((ka + size_ka - d) % size_ka, ka).wait_recv())
        correlation = correlations[step, 0]
        for z in range(1, size_ka):
            correlation = correlation + correlations[step, z]
        correlation = jnp.concatenate([correlation[:, :vectors], correlation[:, vectors:]], axis=0)
        inverse = inverse_factor(correlation * (1.0 / total_rows))
        if step + 1 < STEPS:
            inverse_rows[...] = inverse
        else:
            subspace[...] = jnp.dot(
                inverse, jnp.concatenate([padding, whole], axis=0),
                precision=lax.Precision.HIGHEST, preferred_element_type=F32,
            )
        if step + 1 < STEPS:
            @pl.when(ka != owner)
            def _():
                image_move(ka).wait_recv()

            for f in range(far):
                far_bf16[f] = jnp.dot(
                    inverse,
                    jnp.concatenate([padding[:, :side], far_image[step, f]], axis=0),
                    precision=lax.Precision.HIGHEST, preferred_element_type=F32,
                ).astype(BF16)

            @pl.when(ka == owner)
            def _():
                loop(1, size_ka, lambda d: image_move((ka + d) % size_ka).wait_send())
        loop(1, size_kp, lambda d: rs_move(kp, (kp + d) % size_kp).wait_send())
        loop(1, size_kp, lambda d: ag_move(kp, (kp + d) % size_kp).wait_send())
        loop(1, size_ka, lambda d: c_move(ka, (ka + d) % size_ka).wait_send())

    def finish_plane(n, carry):
        z, e = n // (chips - 1), n % (chips - 1) + 1
        plane_move(z, chip, (chip + e) % chips).wait_send()
        return carry

    lax.fori_loop(0, size_ka * (chips - 1), finish_plane, 0)

    def finish_z(d, carry):
        z_move(ka, (ka + d) % size_ka).wait_send()
        return carry

    lax.fori_loop(1, size_ka, finish_z, 0)
    for i in range(len(sent)):
        @pl.when(goes_up)
        def _():
            far_move(i, up_sem, above).wait_send()

        @pl.when(goes_down)
        def _():
            far_move(i, down_sem, below).wait_send()


def on_device(band_form, interp_coef, screen, coulomb, shift_map, grid_order, energies, initial):
    size_ka = lax.axis_size("ka")
    size_kp = lax.axis_size("kp")
    near, bands, waves = band_form.shape
    side = interp_coef.shape[1]
    rows, vectors = initial.shape
    per_owner, _, group = screen.shape
    far = near * size_ka // size_kp
    pairs = near * far
    chips = size_kp // 2
    width = rows // (size_kp // (vectors // 8))
    dma = pltpu.SemaphoreType.DMA
    kernel, subspace = pl.pallas_call(
        functools.partial(whole_kernel, size_ka, size_kp),
        out_shape=(
            jax.ShapeDtypeStruct((rows, far * side), BF16),
            jax.ShapeDtypeStruct((vectors, rows), F32),
        ),
        in_specs=[SMEM] + [VMEM] * 7,
        out_specs=(VMEM, VMEM),
        scratch_shapes=[
            pltpu.VMEM((far, bands, waves), BF16),
            pltpu.VMEM((far, side, side), BF16),
            pltpu.VMEM((far, vectors, side), BF16),
            pltpu.VMEM((size_ka, waves, per_owner * group), BF16),
            pltpu.VMEM((far, waves // DEPTH * bands, DEPTH), BF16),
            pltpu.VMEM((near, NV // 2 + NC, SUB, waves), BF16),
            pltpu.VMEM((pairs, NC * NC, waves), BF16),
            pltpu.VMEM((pairs, NV * NV, waves), BF16),
            pltpu.VMEM((pairs * NV * NV, NC * NC), F32),
            pltpu.VMEM((pairs * side, LANES), F32),
            pltpu.VMEM((vectors, 2 * vectors), F32),
            pltpu.VMEM((STEPS, vectors, rows), F32),
            pltpu.VMEM((STEPS, vectors, rows), F32),
            pltpu.VMEM((STEPS, far, vectors, side), F32),
            pltpu.VMEM((far, vectors, side), BF16),
            pltpu.VMEM((STEPS, size_kp, 8, width), F32),
            pltpu.VMEM((STEPS, size_ka, vectors // 2, 2 * vectors), F32),
            dma((2 * far + 2,)), dma((2 * far + 2,)), dma((2 * far + 2,)),
            dma((size_ka,)), dma((size_ka,)),
            dma((size_ka, chips)), dma((size_ka, chips)),
            dma((size_ka, chips)), dma((size_ka, chips)),
            dma((STEPS, size_kp)), dma((STEPS, size_kp)),
            dma((STEPS, size_kp)), dma((STEPS, size_kp)),
            dma((STEPS, size_ka)), dma((STEPS, size_ka)),
            dma((STEPS, size_ka)), dma((STEPS,)),
        ],
        compiler_params=pltpu.CompilerParams(
            collective_id=0, has_side_effects=True, vmem_limit_bytes=56 * 2**20
        ),
    )(
        grid_order, band_form, interp_coef, screen.transpose(0, 2, 1), coulomb[None, :], shift_map,
        energies[None, :], initial.T,
    )
    return kernel, subspace.T


def solution(mesh):
    return jax.shard_map(
        on_device,
        mesh=mesh,
        in_specs=(
            P("ka", None, None),
            P("ka", None, None),
            P("ka", "kp", None),
            P(),
            P(),
            P(),
            P("ka"),
            P("ka", None),
        ),
        out_specs=(P("ka", "kp"), P("ka", None)),
        check_vma=False,
    )
```

```python
import functools

import jax
import jax.numpy as jnp
from jax import lax
from jax.experimental import pallas as pl
from jax.experimental.pallas import tpu as pltpu
from jax.sharding import PartitionSpec as P

NV = 8
NC = 16
STEPS = 2
GRID_Y = 8
LANES = 128
DEPTH = 256
CHUNK = 512
SUB = 16
MESH = pl.DeviceIdType.MESH
VMEM = pl.BlockSpec(memory_space=pltpu.VMEM)
SMEM = pl.BlockSpec(memory_space=pltpu.SMEM)
NT = (((1,), (1,)), ((), ()))
TN = (((0,), (0,)), ((), ()))
F32 = jnp.float32
BF16 = jnp.bfloat16


def log2(size):
    return size.bit_length() - 1


def inverse_factor(matrix):
    size = matrix.shape[0]
    work = jnp.concatenate([matrix, jnp.zeros_like(matrix)], axis=1)
    row = lax.broadcasted_iota(jnp.int32, work.shape, 0)
    lane = lax.broadcasted_iota(jnp.int32, work.shape, 1)
    work = jnp.where(lane == row + size, 1.0, work)
    for j in range(0, size, 2):
        first, second = work[j : j + 1, :], work[j + 1 : j + 2, :]
        corner, above, beside, pivot = (
            jnp.broadcast_to(line[:, at : at + 1], line.shape)
            for line, at in ((first, j), (first, j + 1), (second, j), (second, j + 1))
        )
        first_inverse = 1.0 / corner
        ratio = beside * first_inverse
        second = second - ratio * first
        second_scaled = second * (1.0 / (pivot - ratio * above))
        first_scaled = first * first_inverse - ratio * second_scaled
        update = work[:, j : j + 1] * first_scaled + work[:, j + 1 : j + 2] * second_scaled
        work = jnp.where(row > j + 1, work - update, jnp.where(row == j + 1, second, work))
    diagonal = jnp.sum(jnp.where(lane == row, work, 0.0), axis=1, keepdims=True)
    return jnp.where(lane >= size, work * lax.rsqrt(diagonal), 0.0)


def whole_kernel(
    size_ka, size_kp,
    grid_order, form, coef, screen, coulomb, shift_map, energies, initial,
    kernel, subspace,
    far_form, far_coef, far_start, all_cols, source, near_rows, conductions, valences, direct, packed, inverse_rows,
    product, image, far_image, far_bf16, received, correlations,
    up_sem, down_sem, far_sem, z_send, z_recv, plane_send, plane_recv, core_send, core_recv,
    rs_send, rs_recv, ag_send, ag_recv, c_send, c_recv, far_send, far_recv,
):
    ka, kp = lax.axis_index("ka"), lax.axis_index("kp")
    chips = size_kp // 2
    chip, core = kp // 2, kp % 2
    near, far = form.shape[0], far_form.shape[0]
    owner = kp * far // near
    offset = kp * far % near
    per_owner, group, cut = screen.shape
    waves = form.shape[2]
    pieces = waves // DEPTH
    bands = NV + NC
    side = NV * NC
    pairs = near * far
    grid_x = near * size_ka // GRID_Y

    barrier = pltpu.get_barrier_semaphore()

    def greet_z(d, carry):
        pl.semaphore_signal(barrier, inc=1, device_id={"ka": (ka + d) % size_ka}, device_id_type=MESH)
        return carry

    def greet_plane(d, carry):
        pl.semaphore_signal(barrier, inc=1, device_id={"kp": (kp + d) % size_kp}, device_id_type=MESH)
        return carry

    lax.fori_loop(1, size_ka, greet_z, 0)
    lax.fori_loop(1, size_kp, greet_plane, 0)

    @pl.when(ka == owner)
    def _():
        far_form[...] = form[pl.ds(offset, far)]
        far_coef[...] = coef[pl.ds(offset, far)]
        for f in range(far):
            far_start[f] = initial[
                :, pl.ds(pl.multiple_of((offset + f) * side, side), side)
            ].astype(BF16)

    def part(z, p):
        return all_cols.at[z, pl.ds(pl.multiple_of(p * cut, cut), cut), :]

    all_cols[ka, pl.ds(pl.multiple_of(kp * cut, cut), cut), :] = (
        screen[...].reshape(per_owner * group, cut).astype(F32).T.astype(BF16)
    )
    pl.semaphore_wait(barrier, size_ka - 1 + size_kp - 1)

    half_waves = waves // 2
    sent = [
        far_form.at[f, :, h * half_waves : (h + 1) * half_waves]
        for f in range(far)
        for h in range(2)
    ] + [far_coef, far_start]
    forms = 2 * far

    def far_move(i, sem, target):
        return pltpu.make_async_remote_copy(
            src_ref=sent[i], dst_ref=sent[i], send_sem=sem.at[i], recv_sem=far_sem.at[i],
            device_id={"ka": target}, device_id_type=MESH,
        )

    goes_up = (ka >= owner) & (ka < size_ka - 1)
    goes_down = (ka <= owner) & (ka > 0)
    above, below = (ka + 1) % size_ka, (ka + size_ka - 1) % size_ka

    def z_move(z, target):
        return pltpu.make_async_remote_copy(
            src_ref=part(z, kp), dst_ref=part(z, kp), send_sem=z_send.at[target],
            recv_sem=z_recv.at[z], device_id={"ka": target}, device_id_type=MESH,
        )

    def plane_move(z, c, target):
        ref = part(z, c * 2 + core)
        return pltpu.make_async_remote_copy(
            src_ref=ref, dst_ref=ref, send_sem=plane_send.at[z, target],
            recv_sem=plane_recv.at[z, c],
            device_id={"kp": target * 2 + core}, device_id_type=MESH,
        )

    def core_move(z, c, from_core):
        ref = part(z, c * 2 + from_core)
        return pltpu.make_async_remote_copy(
            src_ref=ref, dst_ref=ref, send_sem=core_send.at[z, c], recv_sem=core_recv.at[z, c],
            device_id={"kp": chip * 2 + 1 - core}, device_id_type=MESH,
        )

    def spread(z):
        def to_plane(d, carry):
            plane_move(z, chip, (chip + d) % chips).start()
            return carry

        lax.fori_loop(1, chips, to_plane, 0)
        core_move(z, chip, core).start()

    def forward(i):
        @pl.when(goes_up)
        def _():
            far_move(i, up_sem, above).start()

        @pl.when(goes_down)
        def _():
            far_move(i, down_sem, below).start()

    @pl.when(ka == owner)
    def _():
        for i in range(forms):
            forward(i)

    def to_z(d, carry):
        z_move(ka, (ka + d) % size_ka).start()
        return carry

    lax.fori_loop(1, size_ka, to_z, 0)

    spread(ka)

    def spread_near(k, carry):
        wide = form[k].astype(F32)
        for v in range(0, NV, 2):
            near_rows[k, v // 2] = jnp.concatenate(
                [jnp.broadcast_to(wide[v + i : v + i + 1], (NV, waves)) for i in range(2)], axis=0
            ).astype(BF16)
        for c in range(NC):
            near_rows[k, NV // 2 + c] = jnp.broadcast_to(
                wide[NV + c : NV + c + 1], (NC, waves)
            ).astype(BF16)
        return carry

    lax.fori_loop(0, near, spread_near, 0)

    def relay(first, last):
        @pl.when(ka != owner)
        def _():
            for i in range(first, last):
                far_move(i, up_sem, above).wait_recv()
                forward(i)

    relay(0, 2)

    def from_z(d, carry):
        z = (ka + size_ka - d) % size_ka
        z_move(z, above).wait_recv()
        spread(z)
        return carry

    def from_plane(d, carry):
        z = (ka + size_ka - d) % size_ka

        def one(e, inner):
            c = (chip + chips - e) % chips
            plane_move(z, c, (chip + e) % chips).wait_recv()
            core_move(z, c, core).start()
            return inner

        return lax.fori_loop(1, chips, one, carry)

    def stack(f):
        wide = far_form[f].astype(F32)
        source[f] = jnp.concatenate(
            [wide[:, h * DEPTH : (h + 1) * DEPTH] for h in range(pieces)], axis=0
        ).astype(BF16)

    stack(0)
    lax.fori_loop(1, size_ka, from_z, 0)

    def transfer(k, f):
        near_cell = grid_order[ka * near + k]
        far_cell = grid_order[kp * far + f]
        step_x = (near_cell // GRID_Y - far_cell // GRID_Y + grid_x) % grid_x
        step_y = (near_cell % GRID_Y - far_cell % GRID_Y + GRID_Y) % GRID_Y
        return step_x * GRID_Y + step_y

    plane_steps = -(-size_ka // 4)
    first_plane = pairs - 6
    square = NV * NV

    steps = lax.broadcasted_iota(jnp.int32, (SUB, CHUNK), 0)
    one, zero = jnp.ones((SUB, CHUNK), BF16), jnp.zeros((SUB, CHUNK), BF16)

    def one_pair(n, carry):
        f, k = n // near, n % near
        slot = k * far + f
        q = transfer(k, f)
        total = jnp.zeros((square, NC * NC), F32)
        for s in range(0, waves, CHUNK):
            index = shift_map[pl.ds(q, 1), s : s + CHUNK]
            low = jnp.broadcast_to(index & (DEPTH - 1), (SUB, CHUNK)).astype(F32).astype(BF16)
            high = index >> log2(DEPTH)
            one_hot = jnp.concatenate(
                [
                    jnp.where((steps + r).astype(F32).astype(BF16) == low, one, zero)
                    for r in range(0, DEPTH, SUB)
                ],
                axis=0,
            )
            columns = jnp.dot(source[f], one_hot, preferred_element_type=F32)
            mapped = columns[0:bands]
            for h in range(1, pieces):
                mapped = jnp.where(high == h, columns[h * bands : (h + 1) * bands], mapped)
            top = mapped[0:NV]
            top = jnp.concatenate([top, top], axis=0).astype(BF16)
            rest = mapped[NV:].astype(BF16)
            valence = jnp.concatenate(
                [near_rows[k, i, :, s : s + CHUNK] * top for i in range(NV // 2)], axis=0
            )
            conduction = jnp.concatenate(
                [near_rows[k, NV // 2 + c, :, s : s + CHUNK] * rest for c in range(NC)], axis=0
            )
            valences[slot, :, s : s + CHUNK] = valence
            conductions[slot, :, s : s + CHUNK] = conduction
            scaled = (coulomb[:, s : s + CHUNK] * valence.astype(F32)).astype(BF16)
            total += lax.dot_general(scaled, conduction, NT, preferred_element_type=F32)
        direct[pl.ds(pl.multiple_of(slot * square, square), square), :] = total

        for after in range(1, far):
            @pl.when(n == after - 1)
            def _():
                relay(2 * after, 2 * after + 2)
                stack(after)

        @pl.when(n == far - 1)
        def _():
            @pl.when(ka == owner)
            def _():
                for i in range(forms, forms + 2):
                    forward(i)

            relay(forms, forms + 2)

        @pl.when((n >= first_plane) & (n < first_plane + 4))
        def _():
            low_d = (n - first_plane) * plane_steps
            lax.fori_loop(low_d, jnp.minimum(low_d + plane_steps, size_ka), from_plane, 0)

        return carry

    lax.fori_loop(0, pairs, one_pair, 0)

    def finish(n, carry):
        z, c = n // chips, n % chips
        core_move(z, c, 1 - core).wait_recv()
        core_move(z, c, core).wait_send()
        return carry

    lax.fori_loop(0, size_ka * chips, finish, 0)

    def screening(k, carry):
        for f in range(far):
            n = k * far + f
            q = transfer(k, f)
            columns = all_cols[q // per_owner]
            left = jnp.dot(conductions[n], columns, preferred_element_type=F32)
            right = jnp.dot(valences[n], columns, preferred_element_type=F32)
            lane = lax.broadcasted_iota(jnp.int32, right.shape, 1)
            right = jnp.where((lane >> log2(group)) == q % per_owner, right, 0.0)
            at = pl.ds(pl.multiple_of(n * square, square), square)
            direct[at, :] += lax.dot_general(
                right.astype(BF16), left.astype(BF16), NT, preferred_element_type=F32
            )
        return carry

    lax.fori_loop(0, near, screening, 0)

    all_rows = pairs * square
    row = lax.broadcasted_iota(jnp.int32, (all_rows, LANES), 0)
    lane = lax.broadcasted_iota(jnp.int32, (all_rows, LANES), 1)
    keep = (row & (NV - 1)) == (lane >> log2(NC))
    sum_row = lax.broadcasted_iota(jnp.int32, (pairs * NV, all_rows), 0)
    sum_col = lax.broadcasted_iota(jnp.int32, (pairs * NV, all_rows), 1)
    sums = jnp.where((sum_col >> log2(NV)) == sum_row, 1.0, 0.0).astype(BF16)
    pick_row = lax.broadcasted_iota(jnp.int32, (LANES, LANES), 0)
    pick_lane = lax.broadcasted_iota(jnp.int32, (LANES, LANES), 1)
    per_half = LANES // NC
    same = (pick_row & (NC - 1)) == (pick_lane & (NC - 1))
    for c in range(NC):
        pick = jnp.where(
            ((pick_row >> log2(NC)) == c % per_half) & same, 1.0, 0.0
        ).astype(BF16)
        half_at = c // per_half * LANES
        wide = jnp.dot(
            direct[:, half_at : half_at + LANES].astype(BF16), pick, preferred_element_type=F32
        )
        wide = jnp.where(keep, wide, 0.0).astype(BF16)
        packed[pl.ds(c, pairs * NV, stride=NC), :] = jnp.dot(
            sums, wide, preferred_element_type=F32
        )
    for k in range(near):
        for f in range(far):
            at = (k * far + f) * side
            block = packed[at : at + side, :].astype(BF16)
            half = jnp.dot(block, far_coef[f], preferred_element_type=F32).astype(BF16)
            kernel[k * side : (k + 1) * side, f * side : (f + 1) * side] = lax.dot_general(
                coef[k], half, TN, preferred_element_type=F32
            ).astype(BF16)

    vectors, rows = initial.shape
    half = vectors // 2
    row_groups = vectors // 8
    lane_groups = size_kp // row_groups
    width = rows // lane_groups
    total_rows = rows * size_ka

    def chunk(p):
        return (
            pl.ds(pl.multiple_of(p // lane_groups * 8, 8), 8),
            pl.ds(pl.multiple_of(p % lane_groups * width, width), width),
        )

    own_rows, own_lanes = chunk(kp)
    padding = jnp.zeros((vectors, rows), F32)

    for step in range(STEPS):
        def rs_move(source, target):
            return pltpu.make_async_remote_copy(
                src_ref=product.at[step].at[chunk(target)],
                dst_ref=received.at[step, source],
                send_sem=rs_send.at[step, target], recv_sem=rs_recv.at[step, source],
                device_id={"kp": target}, device_id_type=MESH,
            )

        def ag_move(source, target):
            ref = image.at[step].at[chunk(source)]
            return pltpu.make_async_remote_copy(
                src_ref=ref, dst_ref=ref,
                send_sem=ag_send.at[step, target], recv_sem=ag_recv.at[step, source],
                device_id={"kp": target}, device_id_type=MESH,
            )

        def c_move(source, target):
            ref = correlations.at[step, source]
            return pltpu.make_async_remote_copy(
                src_ref=ref, dst_ref=ref,
                send_sem=c_send.at[step, target], recv_sem=c_recv.at[step, source],
                device_id={"ka": target}, device_id_type=MESH,
            )

        def image_move(target):
            return pltpu.make_async_remote_copy(
                src_ref=far_image.at[step], dst_ref=far_image.at[step],
                send_sem=far_send.at[step, target], recv_sem=far_recv.at[step],
                device_id={"ka": target}, device_id_type=MESH,
            )

        def loop(first, count, body):
            def one(d, carry):
                body(d)
                return carry

            lax.fori_loop(first, count, one, 0)

        total = jnp.zeros((vectors, rows), F32)
        for f in range(far):
            far_vectors = far_start[f] if step == 0 else far_bf16[f]
            total += lax.dot_general(
                far_vectors, kernel[:, f * side : (f + 1) * side], NT, preferred_element_type=F32
            )
        product[step] = total
        loop(1, size_kp, lambda d: rs_move(kp, (kp + d) % size_kp).start())
        received[step, kp] = product[step, own_rows, own_lanes]
        if step == 0:
            current = initial[own_rows, own_lanes]
        else:
            current = jnp.dot(
                inverse_rows[own_rows, :],
                jnp.concatenate(
                    [padding[:, :width], image[step - 1, :, own_lanes]], axis=0
                ),
                precision=lax.Precision.HIGHEST, preferred_element_type=F32,
            )
        loop(1, size_kp, lambda d: rs_move((kp + size_kp - d) % size_kp, kp).wait_recv())
        value = energies[:, own_lanes] * current
        image[step, own_rows, own_lanes] = value + jnp.sum(received[step], axis=0)
        loop(1, size_kp, lambda d: ag_move(kp, (kp + d) % size_kp).start())
        loop(1, size_kp, lambda d: ag_move((kp + size_kp - d) % size_kp, kp).wait_recv())
        whole = image[step]
        local = lax.dot_general(
            whole, whole, NT, precision=lax.Precision.HIGHEST, preferred_element_type=F32
        )
        correlations[step, ka] = jnp.concatenate([local[:half], local[half:]], axis=1)
        loop(1, size_ka, lambda d: c_move(ka, (ka + d) % size_ka).start())
        if step + 1 < STEPS:
            @pl.when(ka == owner)
            def _():
                for f in range(far):
                    far_image[step, f] = image[
                        step, :, pl.ds(pl.multiple_of((offset + f) * side, side), side)
                    ]
                loop(1, size_ka, lambda d: image_move((ka + d) % size_ka).start())
        loop(1, size_ka, lambda d: c_move((ka + size_ka - d) % size_ka, ka).wait_recv())
        correlation = correlations[step, 0]
        for z in range(1, size_ka):
            correlation = correlation + correlations[step, z]
        correlation = jnp.concatenate([correlation[:, :vectors], correlation[:, vectors:]], axis=0)
        inverse = inverse_factor(correlation * (1.0 / total_rows))
        if step + 1 < STEPS:
            inverse_rows[...] = inverse
        else:
            subspace[...] = jnp.dot(
                inverse, jnp.concatenate([padding, whole], axis=0),
                precision=lax.Precision.HIGHEST, preferred_element_type=F32,
            )
        if step + 1 < STEPS:
            @pl.when(ka != owner)
            def _():
                image_move(ka).wait_recv()

            for f in range(far):
                far_bf16[f] = jnp.dot(
                    inverse,
                    jnp.concatenate([padding[:, :side], far_image[step, f]], axis=0),
                    precision=lax.Precision.HIGHEST, preferred_element_type=F32,
                ).astype(BF16)

            @pl.when(ka == owner)
            def _():
                loop(1, size_ka, lambda d: image_move((ka + d) % size_ka).wait_send())
        loop(1, size_kp, lambda d: rs_move(kp, (kp + d) % size_kp).wait_send())
        loop(1, size_kp, lambda d: ag_move(kp, (kp + d) % size_kp).wait_send())
        loop(1, size_ka, lambda d: c_move(ka, (ka + d) % size_ka).wait_send())

    def finish_plane(n, carry):
        z, e = n // (chips - 1), n % (chips - 1) + 1
        plane_move(z, chip, (chip + e) % chips).wait_send()
        return carry

    lax.fori_loop(0, size_ka * (chips - 1), finish_plane, 0)

    def finish_z(d, carry):
        z_move(ka, (ka + d) % size_ka).wait_send()
        return carry

    lax.fori_loop(1, size_ka, finish_z, 0)
    for i in range(len(sent)):
        @pl.when(goes_up)
        def _():
            far_move(i, up_sem, above).wait_send()

        @pl.when(goes_down)
        def _():
            far_move(i, down_sem, below).wait_send()


def on_device(band_form, interp_coef, screen, coulomb, shift_map, grid_order, energies, initial):
    size_ka = lax.axis_size("ka")
    size_kp = lax.axis_size("kp")
    near, bands, waves = band_form.shape
    side = interp_coef.shape[1]
    rows, vectors = initial.shape
    per_owner, _, group = screen.shape
    far = near * size_ka // size_kp
    pairs = near * far
    chips = size_kp // 2
    width = rows // (size_kp // (vectors // 8))
    dma = pltpu.SemaphoreType.DMA
    kernel, subspace = pl.pallas_call(
        functools.partial(whole_kernel, size_ka, size_kp),
        out_shape=(
            jax.ShapeDtypeStruct((rows, far * side), BF16),
            jax.ShapeDtypeStruct((vectors, rows), F32),
        ),
        in_specs=[SMEM] + [VMEM] * 7,
        out_specs=(VMEM, VMEM),
        scratch_shapes=[
            pltpu.VMEM((far, bands, waves), BF16),
            pltpu.VMEM((far, side, side), BF16),
            pltpu.VMEM((far, vectors, side), BF16),
            pltpu.VMEM((size_ka, waves, per_owner * group), BF16),
            pltpu.VMEM((far, waves // DEPTH * bands, DEPTH), BF16),
            pltpu.VMEM((near, NV // 2 + NC, SUB, waves), BF16),
            pltpu.VMEM((pairs, NC * NC, waves), BF16),
            pltpu.VMEM((pairs, NV * NV, waves), BF16),
            pltpu.VMEM((pairs * NV * NV, NC * NC), F32),
            pltpu.VMEM((pairs * side, LANES), F32),
            pltpu.VMEM((vectors, 2 * vectors), F32),
            pltpu.VMEM((STEPS, vectors, rows), F32),
            pltpu.VMEM((STEPS, vectors, rows), F32),
            pltpu.VMEM((STEPS, far, vectors, side), F32),
            pltpu.VMEM((far, vectors, side), BF16),
            pltpu.VMEM((STEPS, size_kp, 8, width), F32),
            pltpu.VMEM((STEPS, size_ka, vectors // 2, 2 * vectors), F32),
            dma((2 * far + 2,)), dma((2 * far + 2,)), dma((2 * far + 2,)),
            dma((size_ka,)), dma((size_ka,)),
            dma((size_ka, chips)), dma((size_ka, chips)),
            dma((size_ka, chips)), dma((size_ka, chips)),
            dma((STEPS, size_kp)), dma((STEPS, size_kp)),
            dma((STEPS, size_kp)), dma((STEPS, size_kp)),
            dma((STEPS, size_ka)), dma((STEPS, size_ka)),
            dma((STEPS, size_ka)), dma((STEPS,)),
        ],
        compiler_params=pltpu.CompilerParams(
            collective_id=0, has_side_effects=True, vmem_limit_bytes=56 * 2**20
        ),
    )(
        grid_order, band_form, interp_coef, screen.transpose(0, 2, 1), coulomb[None, :], shift_map,
        energies[None, :], initial.T,
    )
    return kernel, subspace.T


def solution(mesh):
    return jax.shard_map(
        on_device,
        mesh=mesh,
        in_specs=(
            P("ka", None, None),
            P("ka", None, None),
            P("ka", "kp", None),
            P(),
            P(),
            P(),
            P("ka"),
            P("ka", None),
        ),
        out_specs=(P("ka", "kp"), P("ka", None)),
        check_vma=False,
    )
```
